256 devices in a mesh: bus: 16 (over z_hi, x, core), line: 16 (over y, z_lo).
Axes of the slice: x: 4, y: 4, z: 8 (z_hi: 2, z_lo: 4; z = z_hi * 4 + z_lo), core: 2. Of those that a mesh axis runs over, the one named last changes fastest.
Arguments:
- xrows: bfloat16 [2048, 81920], P('line', 'bus')
- inject: bfloat16 [81920, 96], P('bus'), may hold values from -6 to 6
- line_from: int32 [4096], replicated, may hold values from 0 to 2047
- line_to: int32 [4096], replicated, may hold values from 0 to 2047, as said below
- suscept: float32 [4096], P('line'), may hold values from 1 to 4
- rating: float32 [4096], P('line'), may hold values from 1 to 8
- region_bus: int32 [2048], replicated, may hold values from 0 to 81919, as said below
- outage: int32 [1024], replicated, may hold values from 0 to 4095
Outputs:
- loading: float32 [4096, 1024], P('line', 'bus')
- base_flow: float32 [4096, 96], P('line')
The draws below stay inside these ranges and needn't reach their ends.
Inputs may be any that keep to these rules, and one draw needn't show every extreme that they name: line_to differs from line_from in every line. `region_bus`: all entries differ.
All inputs are finite; a program needn't handle non-finite values.
Results may differ from the reference program's by a relative error of at most 0.0003.
Values may be sent and summed in bfloat16 or wider, within the bound.
A program may use at most 128 MiB of HBM per device.

```python
import math
import jax
import jax.numpy as jnp
import numpy as np
from jax import lax

L_DEV = 256
H = 96
K = 1024
NB = 81920
R = 2048
L = 4096


def region_buses(key):
    key = jax.random.fold_in(key, 101)
    rest = jax.random.permutation(key, NB - 2)[:R - 2].astype(jnp.int32) + 1
    values = jnp.concatenate([jnp.array([0, NB - 1], dtype=jnp.int32), rest])
    order = jax.random.permutation(jax.random.fold_in(key, 7), R)
    return values[order]


def line_ends(key):
    key = jax.random.fold_in(key, 202)
    key_start, key_step = jax.random.split(key)
    first = jax.random.randint(key_start, (L,), 0, R).astype(jnp.int32)
    first = first.at[0].set(0).at[1].set(R - 1)
    offset = jax.random.randint(key_step, (L,), 1, R).astype(jnp.int32)
    offset = offset.at[0].set(R - 1).at[1].set(1)
    return (first, (first + offset) % R)


def draw_region_bus(key, part):
    return region_buses(key)


def draw_line_from(key, part):
    return line_ends(key)[0]


def draw_line_to(key, part):
    return line_ends(key)[1]


def draw_xrows(key, part):
    buses = region_buses(key)
    key = jax.random.fold_in(key, 3)
    key_noise, key_near, key_diag = jax.random.split(key, 3)
    member = jnp.zeros((NB,), jnp.float32).at[buses].set(1.0)
    noise = jax.random.normal(key_noise, (R, NB), jnp.float32)
    background = noise * (1.0 / jnp.sqrt(2.0 * NB))
    near = jax.random.normal(key_near, (R, NB), jnp.float32) * 0.02 * member[None, :]
    diagonal = jnp.exp(jax.random.uniform(key_diag, (R, 1), jnp.float32, jnp.log(0.1), jnp.log(0.35)))
    on_diag = jnp.arange(NB, dtype=jnp.int32)[None, :] == buses[:, None]
    values = background + near + jnp.where(on_diag, diagonal, 0.0)
    return values.astype(jnp.bfloat16)


def touch_ends(values, own_key, smallest, high):
    place = [jax.random.randint(jax.random.fold_in(own_key, axis), (), 0, length) for axis, length in enumerate(values.shape)]
    main_axis = values.shape.index(max(values.shape))
    next_to = place[:main_axis] + [(place[main_axis] + 1) % values.shape[main_axis]] + place[main_axis + 1:]
    return values.at[tuple(place)].set(smallest).at[tuple(next_to)].set(high)


def steps_of(rng, shape, cuts, low, high):
    loudness = 1.0
    for axis_at, parts in cuts:
        draws = jax.random.uniform(jax.random.fold_in(jax.random.fold_in(rng, 6), axis_at), (parts,), jnp.float32, low / len(cuts), high / len(cuts))
        loudness = loudness * jnp.repeat(jnp.exp(draws), shape[axis_at] // parts).reshape((-1,) + (1,) * (len(shape) - 1 - axis_at))
    return loudness


def rank_bounds(count, lean):
    loads = [(1 << 20) // math.isqrt(rank ** lean) + 1 for rank in range(1, count + 1)]
    scale = 1 + sum(loads) // (1 << 30)
    return np.cumsum(np.array([max(1, weight // scale) for weight in loads]))


def skewed_ids(rng, extent, number_of, lean):
    grid = rank_bounds(number_of, lean)
    lot = jax.random.randint(jax.random.fold_in(rng, 1), extent, 0, int(grid[number_of - 1]))
    grade = jnp.searchsorted(jnp.asarray(grid, jnp.int32), lot, side="right")
    return jax.random.permutation(jax.random.fold_in(rng, 2), number_of)[grade].astype(jnp.int32)


def normal_values(rng, shape, width, most, shards=(), kind=jnp.bfloat16):
    drawn = jax.random.normal(rng, shape, jnp.float32) * width
    if len(shards) > 0:
        drawn = steps_of(rng, shape, shards, -0.22, 0.18) * drawn
    return jnp.clip(drawn, min=-most, max=most).astype(kind)


def setup_inputs(seed: int = 0) -> dict:
    streams_of = jax.random.split(jax.random.key(seed), 9)
    return {
        "xrows": draw_xrows(jax.random.fold_in(streams_of[8], 71), 0),
        "inject": normal_values(streams_of[1], (NB, H), 1.0, 6.0, ((0, 16),)),
        "line_from": draw_line_from(jax.random.fold_in(streams_of[8], 71), 0),
        "line_to": draw_line_to(jax.random.fold_in(streams_of[8], 71), 0),
        "suscept": jnp.clip(jnp.exp(math.log(4.0) - 1.3862944 * jax.random.uniform(streams_of[4], (L,), jnp.float32) ** steps_of(streams_of[4], (L,), ((0, 16),), -0.2, 0.2)), 1.0, 4.0),
        "rating": jnp.clip(jnp.exp(math.log(8.0) - 2.0794415 * jax.random.uniform(streams_of[5], (L,), jnp.float32) ** steps_of(streams_of[5], (L,), ((0, 16),), -0.2, 0.2)), 1.0, 8.0),
        "region_bus": draw_region_bus(jax.random.fold_in(streams_of[8], 71), 0),
        "outage": touch_ends(skewed_ids(streams_of[7], (K,), L, 2), jax.random.fold_in(streams_of[7], 3), 0, L - 1).astype(jnp.int32),
    }


def reference(xrows, inject, line_from, line_to, suscept, rating, region_bus, outage):
    ends_from = region_bus[line_from[outage]]
    ends_to = region_bus[line_to[outage]]
    shifted = xrows[:, ends_from].astype(jnp.float32) - xrows[:, ends_to].astype(jnp.float32)
    spread = jnp.dot(xrows, inject, preferred_element_type=jnp.float32)
    sensitivity = suscept[:, None] * (shifted[line_from] - shifted[line_to])
    base_flow = suscept[:, None] * (spread[line_from] - spread[line_to])
    own_term = sensitivity[outage, jnp.arange(K, dtype=jnp.int32)]
    divisor = jnp.maximum(1.0 - own_term, 0.25)
    outage_flow = base_flow[outage]
    scaled_ratio = sensitivity / divisor[None, :]
    blocks = L // L_DEV

    def one_block(pieces):
        ratio_block, flow_block, rating_block = pieces
        post_flow = flow_block[:, None, :] + ratio_block[:, :, None] * outage_flow[None, :, :]
        return jnp.max(jnp.abs(post_flow), axis=2) / rating_block[:, None]

    loading = lax.map(one_block, (scaled_ratio.reshape(blocks, L_DEV, K), base_flow.reshape(blocks, L_DEV, H), rating.reshape(blocks, L_DEV)))
    return loading.reshape(L, K), base_flow
```

```python
import functools

import jax
import jax.numpy as jnp
from jax import lax
from jax.experimental import pallas as pl
from jax.experimental.pallas import tpu as pltpu
from jax.sharding import PartitionSpec as P

MESH = pl.DeviceIdType.MESH
NX, NC, NZH, NY, NZL = 4, 2, 2, 4, 4
HOURS = 12
HPAD = 16
KS = 64
CHUNKS = (32, 32)
OFFS = (0, 32)
WIDTH = (CHUNKS[0] + HPAD, CHUNKS[1])
ROWS = (2 * CHUNKS[0] + HPAD, 2 * CHUNKS[1])


def index_kernel(lines_tiles, bus_loc, outage_ref, from_ref, to_ref, region_ref, out_ref):
    outage = outage_ref[...]
    lo = outage % 128
    hi = outage // 128

    def pick(table_ref, tiles, low, high):
        total = jnp.zeros((8, 128), jnp.int32)
        for t in range(tiles):
            row = jnp.broadcast_to(table_ref[t : t + 1, :], (8, 128))
            got = jnp.take_along_axis(row, low, axis=1, mode="promise_in_bounds")
            total = jnp.where(high == t, got, total)
        return total

    rf = pick(from_ref, 32, lo, hi)
    rt = pick(to_ref, 32, lo, hi)
    start = lax.axis_index("bus") * bus_loc
    ef = pick(region_ref, 16, rf % 128, rf // 128) - start
    et = pick(region_ref, 16, rt % 128, rt // 128) - start
    out_ref[0:8, :] = jnp.where((ef >= 0) & (ef < bus_loc), ef, -512)
    out_ref[8:16, :] = jnp.where((et >= 0) & (et < bus_loc), et, -512)
    out_ref[16:24, :] = rf
    out_ref[24:32, :] = rt
    me = lax.axis_index("line")
    out_ref[32:34, :] = from_ref[pl.ds(me * lines_tiles, lines_tiles), :]
    out_ref[34:36, :] = to_ref[pl.ds(me * lines_tiles, lines_tiles), :]
    out_ref[36:40, :] = jnp.zeros((4, 128), jnp.int32)


def three(v):
    a = v.astype(jnp.bfloat16)
    r = v - a.astype(jnp.float32)
    b = r.astype(jnp.bfloat16)
    c = (r - b.astype(jnp.float32)).astype(jnp.bfloat16)
    return jnp.concatenate([a, b, c], axis=0)


def dot3(parts, rhs, rows):
    d = jnp.dot(parts, rhs, preferred_element_type=jnp.float32)
    return d[0:rows] + d[rows : 2 * rows] + d[2 * rows : 3 * rows]


def main_kernel(
    x_ref, inject_ref, idx_ref, outage_ref, susc2_ref, susc_ref, rating_ref,
    load_ref, base_ref,
    efc, etc, hb, pb0, pb1, ra0, ra1, q0, q1, rb0, rb1, p0, p1, rc0, rc1, full0, full1,
    inc, s4, r4, s0s, s0r, s1s, s1r, s2s, s2r, s3s, s3r, s4s, s4r,
):
    b = lax.axis_index("bus")
    l = lax.axis_index("line")
    zh, x, c = b // 8, (b // 2) % 4, b % 2
    y, zl = l // 4, l % 4
    z = zh * 4 + zl
    bus_loc = x_ref.shape[1]

    def at(zh_, x_, c_, y_, zl_):
        return {"bus": (zh_ * 4 + x_) * 2 + c_, "line": y_ * 4 + zl_}

    group = [((x + dx) % 4, (c + dc) % 2) for dx in range(4) for dc in range(2) if dx or dc]
    zpeers = [(z + dz) % 8 for dz in range(1, 8)]
    zfrom = [(z + 8 - dz) % 8 for dz in range(1, 8)]

    barrier = pltpu.get_barrier_semaphore()
    for gx, gc in group:
        pl.semaphore_signal(barrier, 1, device_id=at(zh, gx, gc, y, zl), device_id_type=MESH)
    for pz in zpeers:
        pl.semaphore_signal(barrier, 1, device_id=at(pz // 4, x, c, y, pz % 4), device_id_type=MESH)
    for dy in range(1, 4):
        pl.semaphore_signal(barrier, 1, device_id=at(zh, x, c, (y + dy) % 4, zl), device_id_type=MESH)

    pb, ra, q, rb, p, rc, full = (pb0, pb1), (ra0, ra1), (q0, q1), (rb0, rb1), (p0, p1), (rc0, rc1), (full0, full1)

    lane = lax.broadcasted_iota(jnp.int32, (128, 128), 1)
    for s in range(8):
        ef = jnp.broadcast_to(idx_ref[s : s + 1, :], (128, 128)).T
        et = jnp.broadcast_to(idx_ref[8 + s : 9 + s, :], (128, 128)).T
        efc[s] = (ef - lane).astype(jnp.int16)
        etc[s] = (et - lane).astype(jnp.int16)

    spread = jnp.dot(x_ref[...], inject_ref[...], preferred_element_type=jnp.float32)
    spread_t = spread.T
    zero4 = jnp.zeros((HPAD - HOURS, 128), jnp.float32)
    for xd in range(4):
        for cd in range(2):
            first = (xd * 2 + cd) * HOURS
            hb[cd, xd] = jnp.concatenate([spread_t[first : first + HOURS], zero4], axis=0)

    one = jnp.bfloat16(1.0)
    minus = jnp.bfloat16(-1.0)
    zero = jnp.bfloat16(0.0)
    step = 1024

    def select(ch, cd):
        k = CHUNKS[ch]
        at_row = pl.multiple_of(cd * 64 + OFFS[ch], 16)
        ef = jnp.concatenate([efc[zd * 4 + xd, pl.ds(at_row, k), :] for xd in range(4) for zd in range(2)], axis=0)
        et = jnp.concatenate([etc[zd * 4 + xd, pl.ds(at_row, k), :] for xd in range(4) for zd in range(2)], axis=0)
        acc = jnp.zeros((8 * k, 128), jnp.float32)
        for t in range(bus_loc // step):
            cols = []
            for u in range(step // 128):
                here = jnp.int16(t * step + u * 128)
                cols.append(jnp.where(ef == here, one, jnp.where(et == here, minus, zero)))
            acc = acc + lax.dot_general(
                jnp.concatenate(cols, axis=1), x_ref[:, t * step : (t + 1) * step],
                (((1,), (1,)), ((), ())), preferred_element_type=jnp.float32,
            )
        for xd in range(4):
            pb[ch][cd, xd, 0 : 2 * k, :] = acc[xd * 2 * k : (xd + 1) * 2 * k]
        if ch == 0:
            for xd in range(4):
                pb[ch][cd, xd, 2 * k : 2 * k + HPAD, :] = hb[cd, xd]

    started = []

    def start(src, dst, ss, rs, where):
        copy = pltpu.make_async_remote_copy(
            src_ref=src, dst_ref=dst, send_sem=ss, recv_sem=rs, device_id=where, device_id_type=MESH
        )
        copy.start()
        started.append(copy)

    def arrived(src, dst, ss, rs):
        pltpu.make_async_remote_copy(
            src_ref=src, dst_ref=dst, send_sem=ss, recv_sem=rs,
            device_id=at(zh, x, 1 - c, y, zl), device_id_type=MESH,
        ).wait_recv()

    def send0(ch):
        start(pb[ch].at[1 - c], ra[ch], s0s.at[ch], s0r.at[ch], at(zh, x, 1 - c, y, zl))

    def send1(ch):
        arrived(pb[ch].at[1 - c], ra[ch], s0s.at[ch], s0r.at[ch])
        q[ch][...] = pb[ch][c] + ra[ch][...]
        for dx in (2, 1, 3):
            px = (x + dx) % 4
            start(q[ch].at[px], rb[ch].at[x], s1s.at[ch, dx], s1r.at[ch, dx], at(zh, px, c, y, zl))

    def send2(ch):
        k = CHUNKS[ch]
        rb[ch][x] = q[ch][x]
        for dx in (1, 3, 2):
            fx = (x + 4 - dx) % 4
            arrived(q[ch].at[fx], rb[ch].at[fx], s1s.at[ch, dx], s1r.at[ch, dx])
        total = (rb[ch][0] + rb[ch][1]) + (rb[ch][2] + rb[ch][3])
        for zd in range(2):
            p[ch][zd, 0:k, :] = total[zd * k : (zd + 1) * k]
        if ch == 0:
            mine = jnp.where(zh == 0, 1.0, 0.0) * susc2_ref[...]
            tail = jnp.concatenate(
                [total[2 * k : 2 * k + HOURS], mine, jnp.zeros((2, 128), jnp.float32)], axis=0
            )
            for zd in range(2):
                p[ch][zd, k : k + HPAD, :] = tail
        for dz in (4, 3, 5, 2, 6, 1, 7):
            pz = (z + dz) % 8
            start(p[ch].at[pz // 4], rc[ch].at[z], s2s.at[ch, dz], s2r.at[ch, dz], at(pz // 4, x, c, y, pz % 4))

    def send3(ch):
        rc[ch][z] = p[ch][zh]
        for dz in (1, 7, 2, 6, 3, 5, 4):
            fz = (z + 8 - dz) % 8
            arrived(p[ch].at[0], rc[ch].at[fz], s2s.at[ch, dz], s2r.at[ch, dz])
        full[ch][y] = rc[ch][0:4] + rc[ch][4:8]
        for dy in (2, 1, 3):
            py = (y + dy) % 4
            start(full[ch].at[y], full[ch].at[y], s3s.at[ch, dy], s3r.at[ch, dy], at(zh, x, c, py, zl))

    def gathered(ch):
        for dy in (1, 3, 2):
            fy = (y + 4 - dy) % 4
            arrived(full[ch].at[y], full[ch].at[fy], s3s.at[ch, dy], s3r.at[ch, dy])

    select(0, 1 - c)
    pl.semaphore_wait(barrier, 17)
    send0(0)
    select(0, c)
    send1(0)
    select(1, 1 - c)
    send0(1)
    select(1, c)
    send1(1)

    for g in range(6):
        if g < 2:
            rf = idx_ref[32 + g : 33 + g, :]
            rt = idx_ref[34 + g : 35 + g, :]
        else:
            rf = idx_ref[pl.ds(16 + zh * 4 + g - 2, 1), :]
            rt = idx_ref[pl.ds(24 + zh * 4 + g - 2, 1), :]
        sub = lax.broadcasted_iota(jnp.int32, (128, 128), 0)
        f16 = (jnp.broadcast_to(rf, (128, 128)) - sub).astype(jnp.int16)
        t16 = (jnp.broadcast_to(rt, (128, 128)) - sub).astype(jnp.int16)
        for r in range(16):
            here = jnp.int16(r * 128)
            inc[r * 128 : (r + 1) * 128, g * 128 : (g + 1) * 128] = jnp.where(
                f16 == here, one, jnp.where(t16 == here, minus, zero)
            )

    send2(0)
    send2(1)
    send3(0)
    send3(1)

    k0 = CHUNKS[0]
    gathered(0)
    hours = jnp.concatenate([full0[i // 4, i % 4, k0 : k0 + HPAD, :] for i in range(16)], axis=1)
    flows = dot3(three(hours), inc[...], HPAD)
    own_flow = flows[:, 0:256] * susc_ref[...]
    for xd in range(4):
        s4[xd, :, 0:256] = own_flow
        s4[xd, :, 256:384] = flows[:, 256 + xd * 128 : 384 + xd * 128]
    for i, (gx, gc) in enumerate(group):
        start(s4.at[gx], r4.at[x * 2 + c], s4s.at[i], s4r.at[i], at(zh, gx, gc, y, zl))
    r4[x * 2 + c] = s4[x]

    row = outage_ref[pl.ds(zh * 4 + x, 1), :]
    table = jnp.concatenate([full0[i // 4, i % 4, k0 + HOURS : k0 + HOURS + 2, :] for i in range(16)], axis=0)
    low = jnp.broadcast_to(row % 128, (128, 128))
    hot = jnp.where(low == lax.broadcasted_iota(jnp.int32, (128, 128), 0), 1.0, 0.0).astype(jnp.bfloat16)
    cand = dot3(three(table), hot, 32)
    high = jnp.broadcast_to(row // 128, (32, 128))
    susc_out = jnp.sum(
        jnp.where(high == lax.broadcasted_iota(jnp.int32, (32, 128), 0), cand, 0.0), axis=0, keepdims=True
    )

    own_inc = inc[:, pl.ds(pl.multiple_of(256 + x * 128, 128), 128)]
    sens, diag = [], []
    for ch in range(2):
        if ch == 1:
            gathered(1)
        k = CHUNKS[ch]
        shifted = three(jnp.concatenate([full[ch][i // 4, i % 4, 0:k, :] for i in range(16)], axis=1))
        sens.append(dot3(shifted, inc[:, 0:256], k))
        diag.append(dot3(shifted, own_inc, k))
    sens = jnp.concatenate(sens, axis=0) * susc_ref[...]
    diag = jnp.concatenate(diag, axis=0) * susc_out
    here = lax.broadcasted_iota(jnp.int32, (KS, 128), 1) == lax.broadcasted_iota(jnp.int32, (KS, 128), 0) + c * KS
    own = jnp.sum(jnp.where(here, diag, 0.0), axis=1, keepdims=True)
    ratio = sens / jnp.maximum(1.0 - own, 0.25)

    for i, (gx, gc) in enumerate(group):
        fx, fc = (x + 4 - (i + 1) // 2) % 4, (c + (i + 1) % 2) % 2
        arrived(s4.at[0], r4.at[fx * 2 + fc], s4s.at[i], s4r.at[i])

    outflow = r4[:, :, 256:384].reshape(128, 128) * susc_out
    outflow = outflow.T
    outflow = jnp.where(c == 0, outflow[0:KS], outflow[KS : 2 * KS])
    worst = jnp.zeros((KS, 256), jnp.float32)
    for s in range(8):
        for h in range(HOURS):
            flow = r4[s, h : h + 1, 0:256]
            col = outflow[:, s * HPAD + h : s * HPAD + h + 1]
            worst = jnp.maximum(worst, jnp.abs(flow + ratio * col))
    load_ref[...] = worst / rating_ref[...]
    for s in range(8):
        base_ref[s * HOURS : (s + 1) * HOURS, :] = r4[s, 0:HOURS, 0:256]

    for copy in started:
        copy.wait_send()


def on_device(xrows, inject, line_from, line_to, suscept, rating, region_bus, outage):
    bus_loc = xrows.shape[1]
    vm = pl.BlockSpec(memory_space=pltpu.VMEM)
    out8 = outage.reshape(8, 128)
    idx = pl.pallas_call(
        functools.partial(index_kernel, 2, bus_loc),
        out_shape=jax.ShapeDtypeStruct((40, 128), jnp.int32),
        in_specs=[vm] * 4,
        out_specs=vm,
        name="indices",
    )(out8, line_from.reshape(32, 128), line_to.reshape(32, 128), region_bus.reshape(16, 128))
    f32, bf16, i16 = jnp.float32, jnp.bfloat16, jnp.int16
    both = lambda lead, counts, kind=f32: [pltpu.VMEM(lead + (n, 128), kind) for n in counts]
    load_t, base_t = pl.pallas_call(
        main_kernel,
        out_shape=(jax.ShapeDtypeStruct((KS, 256), f32), jax.ShapeDtypeStruct((96, 256), f32)),
        in_specs=[vm] * 7,
        out_specs=(vm, vm),
        scratch_shapes=[
            pltpu.VMEM((8, 128, 128), i16),
            pltpu.VMEM((8, 128, 128), i16),
            pltpu.VMEM((2, 4, HPAD, 128), f32),
            *both((2, 4), ROWS),
            *both((4,), ROWS),
            *both((4,), ROWS),
            *both((4,), ROWS),
            *both((2,), WIDTH),
            *both((8,), WIDTH),
            *both((4, 4), WIDTH),
            pltpu.VMEM((2048, 768), bf16),
            pltpu.VMEM((4, HPAD, 384), f32),
            pltpu.VMEM((8, HPAD, 384), f32),
            pltpu.SemaphoreType.DMA((2,)),
            pltpu.SemaphoreType.DMA((2,)),
            pltpu.SemaphoreType.DMA((2, 4)),
            pltpu.SemaphoreType.DMA((2, 4)),
            pltpu.SemaphoreType.DMA((2, 8)),
            pltpu.SemaphoreType.DMA((2, 8)),
            pltpu.SemaphoreType.DMA((2, 4)),
            pltpu.SemaphoreType.DMA((2, 4)),
            pltpu.SemaphoreType.DMA((7,)),
            pltpu.SemaphoreType.DMA((7,)),
        ],
        compiler_params=pltpu.CompilerParams(
            collective_id=0, has_side_effects=True, vmem_limit_bytes=48 * 1024 * 1024
        ),
        name="exchange",
    )(xrows, inject, idx, out8, suscept.reshape(2, 128), suscept.reshape(1, 256), rating.reshape(1, 256))
    return load_t.T, base_t.T


def solution(mesh):
    placed = (P("line", "bus"), P("bus", None), P(), P(), P("line"), P("line"), P(), P())
    return jax.shard_map(
        on_device,
        mesh=mesh,
        in_specs=placed,
        out_specs=(P("line", "bus"), P("line", None)),
        check_vma=False,
    )
```

```python
import jax
import jax.numpy as jnp
from jax import lax
from jax.experimental import pallas as pl
from jax.experimental.pallas import tpu as pltpu
from jax.sharding import PartitionSpec as P

MESH = pl.DeviceIdType.MESH
HOURS = 12
HPAD = 16
KS = 64
CHUNKS = (16, 48)
OFFS = tuple(sum(CHUNKS[:i]) for i in range(len(CHUNKS)))
WIDTH = tuple(k + (HPAD if i == 0 else 0) for i, k in enumerate(CHUNKS))
ROWS = tuple(2 * k + (HPAD if i == 0 else 0) for i, k in enumerate(CHUNKS))
NCH = len(CHUNKS)


def three(v):
    a = v.astype(jnp.bfloat16)
    r = v - a.astype(jnp.float32)
    b = r.astype(jnp.bfloat16)
    c = (r - b.astype(jnp.float32)).astype(jnp.bfloat16)
    return jnp.concatenate([a, b, c], axis=0)


def dot3(parts, rhs, rows):
    d = jnp.dot(parts, rhs, preferred_element_type=jnp.float32)
    return d[0:rows] + d[rows : 2 * rows] + d[2 * rows : 3 * rows]


def lookup(table_ref, tiles, index):
    low, high = index & 127, index >> 7
    total = jnp.zeros((8, 128), jnp.int32)
    for t in range(tiles):
        row = jnp.broadcast_to(table_ref[t : t + 1, :], (8, 128))
        got = jnp.take_along_axis(row, low, axis=1, mode="promise_in_bounds")
        total = jnp.where(high == t, got, total)
    return total


def main_kernel(
    x_hbm, inject_hbm, outage_hbm, from_hbm, to_hbm, region_hbm, susc_hbm, rating_hbm,
    load_ref, base_ref,
    x_ref, inject_ref, outage_ref, from_ref, to_ref, region_ref, susc_ref, rating_ref, in_sem,
    ends, efc, etc, hb, pb, ra, q, rb, p, rc, hfull, sp, rs, inc_flow, inc_sens, s4, r4,
    s0s, s0r, s1s, s1r, s2s, s2r, s3s, s3r, shs, shr, s4s, s4r,
):
    b = lax.axis_index("bus")
    l = lax.axis_index("line")
    zh, x, c = b // 8, (b // 2) % 4, b % 2
    y, zl = l // 4, l % 4
    z = zh * 4 + zl
    bus_loc = x_ref.shape[1]

    loads = [
        pltpu.make_async_copy(src, dst, in_sem.at[i])
        for i, (src, dst) in enumerate((
            (outage_hbm, outage_ref), (from_hbm, from_ref), (to_hbm, to_ref), (region_hbm, region_ref),
            (x_hbm, x_ref), (inject_hbm, inject_ref), (susc_hbm, susc_ref), (rating_hbm, rating_ref),
        ))
    ]
    for load in loads:
        load.start()

    def at(zh_, x_, c_, y_, zl_):
        return {"bus": (zh_ * 4 + x_) * 2 + c_, "line": y_ * 4 + zl_}

    group = [((x + dx) % 4, (c + dc) % 2) for dx in range(4) for dc in range(2) if dx or dc]

    barrier = pltpu.get_barrier_semaphore()
    for dz in range(1, 8):
        pz = (z + dz) % 8
        pl.semaphore_signal(barrier, 1, device_id=at(pz // 4, x, c, y, pz % 4), device_id_type=MESH)
    for gx, gc in group:
        pl.semaphore_signal(barrier, 1, device_id=at(zh, gx, gc, y, zl), device_id_type=MESH)
    for dy in range(1, 4):
        pl.semaphore_signal(barrier, 1, device_id=at(zh, x, c, (y + dy) % 4, zl), device_id_type=MESH)

    for load in loads[:4]:
        load.wait()
    rf = lookup(from_ref, 32, outage_ref[...])
    rt = lookup(to_ref, 32, outage_ref[...])
    ends[0] = rf
    ends[1] = rt
    bus_from = lookup(region_ref, 16, rf) - b * bus_loc
    bus_to = lookup(region_ref, 16, rt) - b * bus_loc
    bus_from = jnp.where((bus_from >= 0) & (bus_from < bus_loc), bus_from, -512)
    bus_to = jnp.where((bus_to >= 0) & (bus_to < bus_loc), bus_to, -512)

    lane = lax.broadcasted_iota(jnp.int32, (128, 128), 1)
    for s in range(8):
        efc[s] = (jnp.broadcast_to(bus_from[s : s + 1, :], (128, 128)).T - lane).astype(jnp.int16)
        etc[s] = (jnp.broadcast_to(bus_to[s : s + 1, :], (128, 128)).T - lane).astype(jnp.int16)

    for load in loads[4:]:
        load.wait()
    spread = lax.dot_general(
        inject_ref[...], x_ref[...], (((1,), (1,)), ((), ())), preferred_element_type=jnp.float32
    )
    zero4 = jnp.zeros((HPAD - HOURS, 128), jnp.float32)
    for xd in range(4):
        for cd in range(2):
            first = (xd * 2 + cd) * HOURS
            hb[cd, xd] = jnp.concatenate([spread[first : first + HOURS], zero4], axis=0)

    one = jnp.bfloat16(1.0)
    minus = jnp.bfloat16(-1.0)
    zero = jnp.bfloat16(0.0)
    step = 1024

    def select(ch, cd):
        k = CHUNKS[ch]
        at_row = pl.multiple_of(cd * 64 + OFFS[ch], 16)
        ef = jnp.concatenate([efc[zd * 4 + xd, pl.ds(at_row, k), :] for xd in range(4) for zd in range(2)], axis=0)
        et = jnp.concatenate([etc[zd * 4 + xd, pl.ds(at_row, k), :] for xd in range(4) for zd in range(2)], axis=0)
        acc = jnp.zeros((8 * k, 128), jnp.float32)
        for t in range(bus_loc // step):
            cols = []
            for u in range(step // 128):
                here = jnp.int16(t * step + u * 128)
                cols.append(jnp.where(ef == here, one, jnp.where(et == here, minus, zero)))
            acc = acc + lax.dot_general(
                jnp.concatenate(cols, axis=1), x_ref[:, t * step : (t + 1) * step],
                (((1,), (1,)), ((), ())), preferred_element_type=jnp.float32,
            )
        for xd in range(4):
            pb[ch][cd, xd, 0 : 2 * k, :] = acc[xd * 2 * k : (xd + 1) * 2 * k]
        if ch == 0:
            for xd in range(4):
                pb[ch][cd, xd, 2 * k : 2 * k + HPAD, :] = hb[cd, xd]

    started = []

    def start(src, dst, ss, rs_, where):
        copy = pltpu.make_async_remote_copy(
            src_ref=src, dst_ref=dst, send_sem=ss, recv_sem=rs_, device_id=where, device_id_type=MESH
        )
        copy.start()
        started.append(copy)

    def arrived(src, dst, ss, rs_):
        pltpu.make_async_remote_copy(
            src_ref=src, dst_ref=dst, send_sem=ss, recv_sem=rs_,
            device_id=at(zh, x, 1 - c, y, zl), device_id_type=MESH,
        ).wait_recv()

    def send0(ch):
        start(pb[ch].at[1 - c], ra[ch], s0s.at[ch], s0r.at[ch], at(zh, x, 1 - c, y, zl))

    def send1(ch):
        arrived(pb[ch].at[1 - c], ra[ch], s0s.at[ch], s0r.at[ch])
        q[ch][...] = pb[ch][c] + ra[ch][...]
        for dx in (2, 1, 3):
            px = (x + dx) % 4
            start(q[ch].at[px], rb[ch].at[x], s1s.at[ch, dx], s1r.at[ch, dx], at(zh, px, c, y, zl))

    def send2(ch):
        k = CHUNKS[ch]
        rb[ch][x] = q[ch][x]
        for dx in (1, 3, 2):
            fx = (x + 4 - dx) % 4
            arrived(q[ch].at[fx], rb[ch].at[fx], s1s.at[ch, dx], s1r.at[ch, dx])
        total = (rb[ch][0] + rb[ch][1]) + (rb[ch][2] + rb[ch][3])
        for zd in range(2):
            p[ch][zd, 0:k, :] = total[zd * k : (zd + 1) * k]
        if ch == 0:
            mine = jnp.where(zh == 0, 1.0, 0.0) * susc_ref[...]
            tail = jnp.concatenate(
                [total[2 * k : 2 * k + HOURS], mine, jnp.zeros((2, 128), jnp.float32)], axis=0
            )
            for zd in range(2):
                p[ch][zd, k : k + HPAD, :] = tail
        for dz in (4, 3, 5, 2, 6, 1, 7):
            pz = (z + dz) % 8
            start(p[ch].at[pz // 4], rc[ch].at[z], s2s.at[ch, dz], s2r.at[ch, dz], at(pz // 4, x, c, y, pz % 4))

    def send3(ch):
        k = CHUNKS[ch]
        rc[ch][z] = p[ch][zh]
        for dz in (1, 7, 2, 6, 3, 5, 4):
            fz = (z + 8 - dz) % 8
            arrived(p[ch].at[0], rc[ch].at[fz], s2s.at[ch, dz], s2r.at[ch, dz])
        if ch == 0:
            hfull[y] = rc[ch][0:4, k : k + HPAD, :] + rc[ch][4:8, k : k + HPAD, :]
            for dy in (2, 1, 3):
                py = (y + dy) % 4
                start(hfull.at[y], hfull.at[y], shs.at[dy], shr.at[dy], at(zh, x, c, py, zl))
        rows = three(jnp.concatenate([rc[ch][i, 0:k, :] + rc[ch][4 + i, 0:k, :] for i in range(4)], axis=1))
        part = dot3(rows, inc_sens[...], k)
        for py in range(4):
            sp[ch][py, 0:k, :] = part[:, py * 256 : (py + 1) * 256]
        diag = (
            lax.broadcasted_iota(jnp.int32, (k, 128), 1)
            == lax.broadcasted_iota(jnp.int32, (k, 128), 0) + (c * KS + OFFS[ch])
        )
        own = jnp.sum(jnp.where(diag, part[:, 1024:1152], 0.0), axis=0, keepdims=True)
        own = jnp.broadcast_to(jnp.concatenate([own, own], axis=1), (8, 256))
        for py in range(4):
            sp[ch][py, k : k + 8, :] = own
        for dy in (2, 1, 3):
            py = (y + dy) % 4
            start(sp[ch].at[py], rs[ch].at[y], s3s.at[ch, dy], s3r.at[ch, dy], at(zh, x, c, py, zl))
        rs[ch][y] = sp[ch][y]

    def hot(from_row, to_row, first):
        sub = lax.broadcasted_iota(jnp.int32, (128, 128), 0) + first
        return (
            (jnp.broadcast_to(from_row, (128, 128)) - sub).astype(jnp.int16),
            (jnp.broadcast_to(to_row, (128, 128)) - sub).astype(jnp.int16),
        )

    def fill(out, g, tiles, from_row, to_row, first):
        f16, t16 = hot(from_row, to_row, first)
        for r in range(tiles):
            here = jnp.int16(r * 128)
            out[r * 128 : (r + 1) * 128, g * 128 : (g + 1) * 128] = jnp.where(
                f16 == here, one, jnp.where(t16 == here, minus, zero)
            )

    select(0, 1 - c)
    pl.semaphore_wait(barrier, 17)
    send0(0)
    select(0, c)
    send1(0)
    for ch in range(1, NCH):
        select(ch, 1 - c)
        send0(ch)
        select(ch, c)
        send1(ch)

    for g in range(8):
        at_line = (g // 2 * 4 + zl) * 2 + g % 2
        fill(inc_sens, g, 4, from_ref[pl.ds(at_line, 1), :], to_ref[pl.ds(at_line, 1), :], y * 512)
    at_tile = zh * 4 + x
    fill(inc_sens, 8, 4, ends[0, pl.ds(at_tile, 1), :], ends[1, pl.ds(at_tile, 1), :], y * 512)
    send2(0)
    for g in range(2):
        fill(inc_flow, g, 16, from_ref[pl.ds(l * 2 + g, 1), :], to_ref[pl.ds(l * 2 + g, 1), :], 0)
    for g in range(4):
        fill(inc_flow, 2 + g, 16, ends[0, pl.ds(zh * 4 + g, 1), :], ends[1, pl.ds(zh * 4 + g, 1), :], 0)
    for ch in range(1, NCH):
        send2(ch)
    for ch in range(NCH):
        send3(ch)

    susc_row = jnp.concatenate([susc_ref[0:1, :], susc_ref[1:2, :]], axis=1)
    for dy in (1, 3, 2):
        fy = (y + 4 - dy) % 4
        arrived(hfull.at[y], hfull.at[fy], shs.at[dy], shr.at[dy])
    hours = jnp.concatenate([hfull[i // 4, i % 4] for i in range(16)], axis=1)
    flows = dot3(three(hours), inc_flow[...], HPAD)
    own_flow = flows[:, 0:256] * susc_row
    for xd in range(4):
        s4[xd, :, 0:256] = own_flow
        s4[xd, :, 256:384] = flows[:, 256 + xd * 128 : 384 + xd * 128]
    for i, (gx, gc) in enumerate(group):
        start(s4.at[gx], r4.at[x * 2 + c], s4s.at[i], s4r.at[i], at(zh, gx, gc, y, zl))
    r4[x * 2 + c] = s4[x]

    row = outage_ref[pl.ds(at_tile, 1), :]
    table = jnp.concatenate([hfull[i // 4, i % 4, HOURS : HOURS + 2, :] for i in range(16)], axis=0)
    low = jnp.broadcast_to(row & 127, (128, 128))
    hit = jnp.where(low == lax.broadcasted_iota(jnp.int32, (128, 128), 0), 1.0, 0.0).astype(jnp.bfloat16)
    cand = dot3(three(table), hit, 32)
    high = jnp.broadcast_to(row >> 7, (32, 128))
    susc_out = jnp.sum(
        jnp.where(high == lax.broadcasted_iota(jnp.int32, (32, 128), 0), cand, 0.0), axis=0, keepdims=True
    )

    sens = []
    own = jnp.zeros((1, 128), jnp.float32)
    for ch in range(NCH):
        k = CHUNKS[ch]
        for dy in (1, 3, 2):
            fy = (y + 4 - dy) % 4
            arrived(sp[ch].at[0], rs[ch].at[fy], s3s.at[ch, dy], s3r.at[ch, dy])
        total = (rs[ch][0] + rs[ch][1]) + (rs[ch][2] + rs[ch][3])
        sens.append(total[0:k])
        own = own + total[k : k + 1, 0:128]
    sens = jnp.concatenate(sens, axis=0) * susc_row
    here = lax.broadcasted_iota(jnp.int32, (KS, 128), 1) == lax.broadcasted_iota(jnp.int32, (KS, 128), 0) + c * KS
    divisor = jnp.maximum(1.0 - own * susc_out, 0.25)
    divisor = jnp.sum(jnp.where(here, jnp.broadcast_to(divisor, (KS, 128)), 0.0), axis=1, keepdims=True)
    ratio = sens / divisor

    for i in range(7):
        fx, fc = (x + 4 - (i + 1) // 2) % 4, (c + (i + 1) % 2) % 2
        arrived(s4.at[0], r4.at[fx * 2 + fc], s4s.at[i], s4r.at[i])

    outflow = r4[:, :, 256:384].reshape(128, 128) * susc_out
    outflow = outflow.T
    outflow = jnp.where(c == 0, outflow[0:KS], outflow[KS : 2 * KS])
    worst = jnp.zeros((KS, 256), jnp.float32)
    for s in range(8):
        for h in range(HOURS):
            flow = r4[s, h : h + 1, 0:256]
            col = outflow[:, s * HPAD + h : s * HPAD + h + 1]
            worst = jnp.maximum(worst, jnp.abs(flow + ratio * col))
    load_ref[...] = worst / jnp.concatenate([rating_ref[0:1, :], rating_ref[1:2, :]], axis=1)
    for s in range(8):
        base_ref[s * HOURS : (s + 1) * HOURS, :] = r4[s, 0:HOURS, 0:256]

    for copy in started:
        copy.wait_send()


def on_device(xrows, inject, line_from, line_to, suscept, rating, region_bus, outage):
    vm = pl.BlockSpec(memory_space=pltpu.VMEM)
    far = pl.BlockSpec(memory_space=pl.ANY)
    f32, bf16, i16, i32 = jnp.float32, jnp.bfloat16, jnp.int16, jnp.int32
    vmem = lambda shape, kind=f32: pltpu.VMEM(shape, kind)
    each = lambda lead, counts, last=128: tuple(pltpu.VMEM(lead + (n, last), f32) for n in counts)
    sems = lambda *shape: pltpu.SemaphoreType.DMA(shape)
    args = (
        xrows, inject.T, outage.reshape(8, 128), line_from.reshape(32, 128), line_to.reshape(32, 128),
        region_bus.reshape(16, 128), suscept.reshape(2, 128), rating.reshape(2, 128),
    )
    sens_rows = tuple(k + 8 for k in CHUNKS)
    load_t, base_t = pl.pallas_call(
        main_kernel,
        out_shape=(jax.ShapeDtypeStruct((KS, 256), f32), jax.ShapeDtypeStruct((96, 256), f32)),
        in_specs=[far] * 8,
        out_specs=(vm, vm),
        scratch_shapes=[
            *[vmem(a.shape, a.dtype) for a in args],
            sems(8),
            vmem((2, 8, 128), i32),
            vmem((8, 128, 128), i16),
            vmem((8, 128, 128), i16),
            vmem((2, 4, HPAD, 128)),
            each((2, 4), ROWS),
            each((4,), ROWS),
            each((4,), ROWS),
            each((4,), ROWS),
            each((2,), WIDTH),
            each((8,), WIDTH),
            vmem((4, 4, HPAD, 128)),
            each((4,), sens_rows, 256),
            each((4,), sens_rows, 256),
            vmem((2048, 768), bf16),
            vmem((512, 1152), bf16),
            vmem((4, HPAD, 384)),
            vmem((8, HPAD, 384)),
            sems(NCH), sems(NCH),
            sems(NCH, 4), sems(NCH, 4),
            sems(NCH, 8), sems(NCH, 8),
            sems(NCH, 4), sems(NCH, 4),
            sems(4), sems(4),
            sems(7), sems(7),
        ],
        compiler_params=pltpu.CompilerParams(
            collective_id=0, has_side_effects=True, vmem_limit_bytes=60 * 1024 * 1024
        ),
        name="exchange",
    )(*args)
    return load_t.T, base_t.T


def solution(mesh):
    placed = (P("line", "bus"), P("bus", None), P(), P(), P("line"), P("line"), P(), P())
    return jax.shard_map(
        on_device,
        mesh=mesh,
        in_specs=placed,
        out_specs=(P("line", "bus"), P("line", None)),
        check_vma=False,
    )
```

```python
import jax
import jax.numpy as jnp
from jax import lax
from jax.experimental import pallas as pl
from jax.experimental.pallas import tpu as pltpu
from jax.sharding import PartitionSpec as P

MESH = pl.DeviceIdType.MESH
HOURS = 12
HPAD = 16
KS = 64
CHUNKS = (32, 32)
OFFS = tuple(sum(CHUNKS[:i]) for i in range(len(CHUNKS)))
ROWS = tuple(2 * k for k in CHUNKS)
NCH = len(CHUNKS)


def three(v):
    a = v.astype(jnp.bfloat16)
    r = v - a.astype(jnp.float32)
    b = r.astype(jnp.bfloat16)
    c = (r - b.astype(jnp.float32)).astype(jnp.bfloat16)
    return jnp.concatenate([a, b, c], axis=0)


def dot3(parts, rhs, rows):
    d = jnp.dot(parts, rhs, preferred_element_type=jnp.float32)
    return d[0:rows] + d[rows : 2 * rows] + d[2 * rows : 3 * rows]


def lookup(table_ref, tiles, index):
    low, high = index & 127, index >> 7
    total = jnp.zeros((8, 128), jnp.int32)
    for t in range(tiles):
        row = jnp.broadcast_to(table_ref[t : t + 1, :], (8, 128))
        got = jnp.take_along_axis(row, low, axis=1, mode="promise_in_bounds")
        total = jnp.where(high == t, got, total)
    return total


def main_kernel(
    x_hbm, inject_hbm, outage_hbm, from_hbm, to_hbm, region_hbm, susc_hbm, rating_hbm,
    out_ref,
    x_ref, inject_ref, outage_ref, from_ref, to_ref, region_ref, susc_ref, rating_ref, in_sem,
    ends, efc, etc, hb, rh, ph, rch, hfull, pb, ra, q, rb, p, rc, sp, rs, inc_flow, inc_sens, s4, r4,
    h1s, h1r, h2s, h2r, h3s, h3r, s0s, s0r, s1s, s1r, s2s, s2r, s3s, s3r, s4s, s4r,
):
    b = lax.axis_index("bus")
    l = lax.axis_index("line")
    zh, x, c = b // 8, (b // 2) % 4, b % 2
    y, zl = l // 4, l % 4
    z = zh * 4 + zl
    bus_loc = x_ref.shape[1]

    loads = [
        pltpu.make_async_copy(src, dst, in_sem.at[i])
        for i, (src, dst) in enumerate((
            (x_hbm, x_ref), (inject_hbm, inject_ref), (outage_hbm, outage_ref), (from_hbm, from_ref),
            (to_hbm, to_ref), (region_hbm, region_ref), (susc_hbm, susc_ref), (rating_hbm, rating_ref),
        ))
    ]
    for load in loads:
        load.start()

    def at(zh_, x_, c_, y_, zl_):
        return {"bus": (zh_ * 4 + x_) * 2 + c_, "line": y_ * 4 + zl_}

    group = [((x + dx) % 4, (c + dc) % 2) for dx in range(4) for dc in range(2) if dx or dc]

    barrier = pltpu.get_barrier_semaphore()
    for dz in range(1, 8):
        pz = (z + dz) % 8
        pl.semaphore_signal(barrier, 1, device_id=at(pz // 4, x, c, y, pz % 4), device_id_type=MESH)
    for gx, gc in group:
        pl.semaphore_signal(barrier, 1, device_id=at(zh, gx, gc, y, zl), device_id_type=MESH)
    for dy in range(1, 4):
        pl.semaphore_signal(barrier, 1, device_id=at(zh, x, c, (y + dy) % 4, zl), device_id_type=MESH)

    started = []

    def start(src, dst, ss, rs_, where):
        copy = pltpu.make_async_remote_copy(
            src_ref=src, dst_ref=dst, send_sem=ss, recv_sem=rs_, device_id=where, device_id_type=MESH
        )
        copy.start()
        started.append(copy)

    def arrived(src, dst, ss, rs_):
        pltpu.make_async_remote_copy(
            src_ref=src, dst_ref=dst, send_sem=ss, recv_sem=rs_,
            device_id=at(zh, x, 1 - c, y, zl), device_id_type=MESH,
        ).wait_recv()

    for load in loads[:2]:
        load.wait()
    spread = lax.dot_general(
        inject_ref[...], x_ref[...], (((1,), (1,)), ((), ())), preferred_element_type=jnp.float32
    )
    zero4 = jnp.zeros((HPAD - HOURS, 128), jnp.float32)
    for xd in range(4):
        for cd in range(2):
            first = (xd * 2 + cd) * HOURS
            hb[cd, xd] = jnp.concatenate([spread[first : first + HOURS], zero4], axis=0)

    pl.semaphore_wait(barrier, 17)
    for i, (gx, gc) in enumerate(group):
        start(hb.at[gc, gx], rh.at[x * 2 + c], h1s.at[i], h1r.at[i], at(zh, gx, gc, y, zl))

    def hours2():
        rh[x * 2 + c] = hb[c, x]
        for i in range(7):
            fx, fc = (x + 4 - (i + 1) // 2) % 4, (c + (i + 1) % 2) % 2
            arrived(hb.at[0, 0], rh.at[fx * 2 + fc], h1s.at[i], h1r.at[i])
        total = ((rh[0] + rh[1]) + (rh[2] + rh[3])) + ((rh[4] + rh[5]) + (rh[6] + rh[7]))
        mine = jnp.where(zh == 0, 1.0, 0.0) * susc_ref[...]
        ph[...] = jnp.concatenate([total[0:HOURS], mine, jnp.zeros((2, 128), jnp.float32)], axis=0)
        for dz in (4, 3, 5, 2, 6, 1, 7):
            pz = (z + dz) % 8
            start(ph, rch.at[z], h2s.at[dz], h2r.at[dz], at(pz // 4, x, c, y, pz % 4))

    def hours3():
        rch[z] = ph[...]
        for dz in (1, 7, 2, 6, 3, 5, 4):
            fz = (z + 8 - dz) % 8
            arrived(ph, rch.at[fz], h2s.at[dz], h2r.at[dz])
        hfull[y] = rch[0:4] + rch[4:8]
        for dy in (2, 1, 3):
            py = (y + dy) % 4
            start(hfull.at[y], hfull.at[y], h3s.at[dy], h3r.at[dy], at(zh, x, c, py, zl))

    for load in loads[2:]:
        load.wait()
    rf = lookup(from_ref, 32, outage_ref[...])
    rt = lookup(to_ref, 32, outage_ref[...])
    ends[0] = rf
    ends[1] = rt
    bus_from = lookup(region_ref, 16, rf) - b * bus_loc
    bus_to = lookup(region_ref, 16, rt) - b * bus_loc
    bus_from = jnp.where((bus_from >= 0) & (bus_from < bus_loc), bus_from, -512)
    bus_to = jnp.where((bus_to >= 0) & (bus_to < bus_loc), bus_to, -512)

    lane = lax.broadcasted_iota(jnp.int32, (128, 128), 1)
    for s in range(8):
        efc[s] = (jnp.broadcast_to(bus_from[s : s + 1, :], (128, 128)).T - lane).astype(jnp.int16)
        etc[s] = (jnp.broadcast_to(bus_to[s : s + 1, :], (128, 128)).T - lane).astype(jnp.int16)

    one = jnp.bfloat16(1.0)
    minus = jnp.bfloat16(-1.0)
    zero = jnp.bfloat16(0.0)
    step = 1024

    def select(ch, cd):
        k = CHUNKS[ch]
        at_row = pl.multiple_of(cd * 64 + OFFS[ch], 16)
        ef = jnp.concatenate([efc[zd * 4 + xd, pl.ds(at_row, k), :] for xd in range(4) for zd in range(2)], axis=0)
        et = jnp.concatenate([etc[zd * 4 + xd, pl.ds(at_row, k), :] for xd in range(4) for zd in range(2)], axis=0)
        acc = jnp.zeros((8 * k, 128), jnp.float32)
        for t in range(bus_loc // step):
            cols = []
            for u in range(step // 128):
                here = jnp.int16(t * step + u * 128)
                cols.append(jnp.where(ef == here, one, jnp.where(et == here, minus, zero)))
            acc = acc + lax.dot_general(
                jnp.concatenate(cols, axis=1), x_ref[:, t * step : (t + 1) * step],
                (((1,), (1,)), ((), ())), preferred_element_type=jnp.float32,
            )
        for xd in range(4):
            pb[ch][cd, xd, 0 : 2 * k, :] = acc[xd * 2 * k : (xd + 1) * 2 * k]

    def send0(ch):
        start(pb[ch].at[1 - c], ra[ch], s0s.at[ch], s0r.at[ch], at(zh, x, 1 - c, y, zl))

    def send1(ch):
        arrived(pb[ch].at[1 - c], ra[ch], s0s.at[ch], s0r.at[ch])
        q[ch][...] = pb[ch][c] + ra[ch][...]
        for dx in (2, 1, 3):
            px = (x + dx) % 4
            start(q[ch].at[px], rb[ch].at[x], s1s.at[ch, dx], s1r.at[ch, dx], at(zh, px, c, y, zl))

    def send2(ch):
        k = CHUNKS[ch]
        rb[ch][x] = q[ch][x]
        for dx in (1, 3, 2):
            fx = (x + 4 - dx) % 4
            arrived(q[ch].at[fx], rb[ch].at[fx], s1s.at[ch, dx], s1r.at[ch, dx])
        total = (rb[ch][0] + rb[ch][1]) + (rb[ch][2] + rb[ch][3])
        for zd in range(2):
            p[ch][zd, 0:k, :] = total[zd * k : (zd + 1) * k]
        for dz in (4, 3, 5, 2, 6, 1, 7):
            pz = (z + dz) % 8
            start(p[ch].at[pz // 4], rc[ch].at[z], s2s.at[ch, dz], s2r.at[ch, dz], at(pz // 4, x, c, y, pz % 4))

    def send3(ch):
        k = CHUNKS[ch]
        rc[ch][z] = p[ch][zh]
        for dz in (1, 7, 2, 6, 3, 5, 4):
            fz = (z + 8 - dz) % 8
            arrived(p[ch].at[0], rc[ch].at[fz], s2s.at[ch, dz], s2r.at[ch, dz])
        rows = three(jnp.concatenate([rc[ch][i, 0:k, :] + rc[ch][4 + i, 0:k, :] for i in range(4)], axis=1))
        part = dot3(rows, inc_sens[...], k)
        for py in range(4):
            sp[ch][py, 0:k, :] = part[:, py * 256 : (py + 1) * 256]
        diag = (
            lax.broadcasted_iota(jnp.int32, (k, 128), 1)
            == lax.broadcasted_iota(jnp.int32, (k, 128), 0) + (c * KS + OFFS[ch])
        )
        own = jnp.sum(jnp.where(diag, part[:, 1024:1152], 0.0), axis=0, keepdims=True)
        own = jnp.broadcast_to(jnp.concatenate([own, own], axis=1), (8, 256))
        for py in range(4):
            sp[ch][py, k : k + 8, :] = own
        for dy in (2, 1, 3):
            py = (y + dy) % 4
            start(sp[ch].at[py], rs[ch].at[y], s3s.at[ch, dy], s3r.at[ch, dy], at(zh, x, c, py, zl))
        rs[ch][y] = sp[ch][y]

    def hot(from_row, to_row, first):
        sub = lax.broadcasted_iota(jnp.int32, (128, 128), 0) + first
        return (
            (jnp.broadcast_to(from_row, (128, 128)) - sub).astype(jnp.int16),
            (jnp.broadcast_to(to_row, (128, 128)) - sub).astype(jnp.int16),
        )

    def fill(out, g, tiles, from_row, to_row, first):
        f16, t16 = hot(from_row, to_row, first)
        for r in range(tiles):
            here = jnp.int16(r * 128)
            out[r * 128 : (r + 1) * 128, g * 128 : (g + 1) * 128] = jnp.where(
                f16 == here, one, jnp.where(t16 == here, minus, zero)
            )

    select(0, 1 - c)
    send0(0)
    select(0, c)
    send1(0)
    for ch in range(1, NCH):
        select(ch, 1 - c)
        send0(ch)
        if ch == 1:
            hours2()
        select(ch, c)
        send1(ch)
    if NCH == 1:
        hours2()

    for g in range(8):
        at_line = (g // 2 * 4 + zl) * 2 + g % 2
        fill(inc_sens, g, 4, from_ref[pl.ds(at_line, 1), :], to_ref[pl.ds(at_line, 1), :], y * 512)
    at_tile = zh * 4 + x
    fill(inc_sens, 8, 4, ends[0, pl.ds(at_tile, 1), :], ends[1, pl.ds(at_tile, 1), :], y * 512)
    for g in range(2):
        fill(inc_flow, g, 16, from_ref[pl.ds(l * 2 + g, 1), :], to_ref[pl.ds(l * 2 + g, 1), :], 0)
    for g in range(4):
        fill(inc_flow, 2 + g, 16, ends[0, pl.ds(zh * 4 + g, 1), :], ends[1, pl.ds(zh * 4 + g, 1), :], 0)
    send2(0)
    hours3()
    for ch in range(1, NCH):
        send2(ch)
    for ch in range(NCH - 1):
        send3(ch)

    susc_row = jnp.concatenate([susc_ref[0:1, :], susc_ref[1:2, :]], axis=1)
    for dy in (1, 3, 2):
        fy = (y + 4 - dy) % 4
        arrived(hfull.at[y], hfull.at[fy], h3s.at[dy], h3r.at[dy])
    hours = jnp.concatenate([hfull[i // 4, i % 4] for i in range(16)], axis=1)
    flows = dot3(three(hours), inc_flow[...], HPAD)
    own_flow = flows[:, 0:256] * susc_row
    for xd in range(4):
        s4[xd, :, 0:256] = own_flow
        s4[xd, :, 256:384] = flows[:, 256 + xd * 128 : 384 + xd * 128]
    for i, (gx, gc) in enumerate(group):
        start(s4.at[gx], r4.at[x * 2 + c], s4s.at[i], s4r.at[i], at(zh, gx, gc, y, zl))
    r4[x * 2 + c] = s4[x]
    send3(NCH - 1)

    row = outage_ref[pl.ds(at_tile, 1), :]
    table = jnp.concatenate([hfull[i // 4, i % 4, HOURS : HOURS + 2, :] for i in range(16)], axis=0)
    low = jnp.broadcast_to(row & 127, (128, 128))
    hit = jnp.where(low == lax.broadcasted_iota(jnp.int32, (128, 128), 0), 1.0, 0.0).astype(jnp.bfloat16)
    cand = dot3(three(table), hit, 32)
    high = jnp.broadcast_to(row >> 7, (32, 128))
    susc_out = jnp.sum(
        jnp.where(high == lax.broadcasted_iota(jnp.int32, (32, 128), 0), cand, 0.0), axis=0, keepdims=True
    )

    sens = []
    own = jnp.zeros((1, 128), jnp.float32)
    for ch in range(NCH):
        k = CHUNKS[ch]
        for dy in (1, 3, 2):
            fy = (y + 4 - dy) % 4
            arrived(sp[ch].at[0], rs[ch].at[fy], s3s.at[ch, dy], s3r.at[ch, dy])
        total = (rs[ch][0] + rs[ch][1]) + (rs[ch][2] + rs[ch][3])
        sens.append(total[0:k])
        own = own + total[k : k + 1, 0:128]
    sens = jnp.concatenate(sens, axis=0) * susc_row
    here = lax.broadcasted_iota(jnp.int32, (KS, 128), 1) == lax.broadcasted_iota(jnp.int32, (KS, 128), 0) + c * KS
    divisor = jnp.maximum(1.0 - own * susc_out, 0.25)
    divisor = jnp.sum(jnp.where(here, jnp.broadcast_to(divisor, (KS, 128)), 0.0), axis=1, keepdims=True)
    ratio = sens / divisor

    for i in range(7):
        fx, fc = (x + 4 - (i + 1) // 2) % 4, (c + (i + 1) % 2) % 2
        arrived(s4.at[0], r4.at[fx * 2 + fc], s4s.at[i], s4r.at[i])

    outflow = r4[:, :, 256:384].reshape(128, 128) * susc_out
    outflow = outflow.T
    outflow = jnp.where(c == 0, outflow[0:KS], outflow[KS : 2 * KS])
    worst = jnp.zeros((KS, 256), jnp.float32)
    for s in range(8):
        for h in range(HOURS):
            flow = r4[s, h : h + 1, 0:256]
            col = outflow[:, s * HPAD + h : s * HPAD + h + 1]
            worst = jnp.maximum(worst, jnp.abs(flow + ratio * col))
    out_ref[0:KS, :] = worst / jnp.concatenate([rating_ref[0:1, :], rating_ref[1:2, :]], axis=1)
    for s in range(8):
        out_ref[KS + s * HOURS : KS + (s + 1) * HOURS, :] = r4[s, 0:HOURS, 0:256]

    for copy in started:
        copy.wait_send()


def split_kernel(both_ref, load_ref, base_ref, here, sem):
    load = pltpu.make_async_copy(both_ref, here, sem.at[2])
    load.start()
    load.wait()
    first = pltpu.make_async_copy(here.at[0:KS, :], load_ref, sem.at[0])
    second = pltpu.make_async_copy(here.at[KS : KS + 96, :], base_ref, sem.at[1])
    first.start()
    second.start()
    first.wait()
    second.wait()


def on_device(xrows, inject, line_from, line_to, suscept, rating, region_bus, outage):
    vm = pl.BlockSpec(memory_space=pltpu.VMEM)
    far = pl.BlockSpec(memory_space=pl.ANY)
    f32, bf16, i16, i32 = jnp.float32, jnp.bfloat16, jnp.int16, jnp.int32
    vmem = lambda shape, kind=f32: pltpu.VMEM(shape, kind)
    each = lambda lead, counts, last=128: tuple(pltpu.VMEM(lead + (n, last), f32) for n in counts)
    sems = lambda *shape: pltpu.SemaphoreType.DMA(shape)
    args = (
        xrows, inject.T, outage.reshape(8, 128), line_from.reshape(32, 128), line_to.reshape(32, 128),
        region_bus.reshape(16, 128), suscept.reshape(2, 128), rating.reshape(2, 128),
    )
    sens_rows = tuple(k + 8 for k in CHUNKS)
    both = pl.pallas_call(
        main_kernel,
        out_shape=jax.ShapeDtypeStruct((KS + 96, 256), f32),
        in_specs=[far] * 8,
        out_specs=vm,
        scratch_shapes=[
            *[vmem(a.shape, a.dtype) for a in args],
            sems(8),
            vmem((2, 8, 128), i32),
            vmem((8, 128, 128), i16),
            vmem((8, 128, 128), i16),
            vmem((2, 4, HPAD, 128)),
            vmem((8, HPAD, 128)),
            vmem((HPAD, 128)),
            vmem((8, HPAD, 128)),
            vmem((4, 4, HPAD, 128)),
            each((2, 4), ROWS),
            each((4,), ROWS),
            each((4,), ROWS),
            each((4,), ROWS),
            each((2,), CHUNKS),
            each((8,), CHUNKS),
            each((4,), sens_rows, 256),
            each((4,), sens_rows, 256),
            vmem((2048, 768), bf16),
            vmem((512, 1152), bf16),
            vmem((4, HPAD, 384)),
            vmem((8, HPAD, 384)),
            sems(7), sems(7),
            sems(8), sems(8),
            sems(4), sems(4),
            sems(NCH), sems(NCH),
            sems(NCH, 4), sems(NCH, 4),
            sems(NCH, 8), sems(NCH, 8),
            sems(NCH, 4), sems(NCH, 4),
            sems(7), sems(7),
        ],
        compiler_params=pltpu.CompilerParams(
            collective_id=0, has_side_effects=True, vmem_limit_bytes=60 * 1024 * 1024
        ),
        name="exchange",
    )(*args)
    load_t, base_t = pl.pallas_call(
        split_kernel,
        out_shape=(jax.ShapeDtypeStruct((KS, 256), f32), jax.ShapeDtypeStruct((96, 256), f32)),
        in_specs=[far],
        out_specs=(far, far),
        scratch_shapes=[vmem((KS + 96, 256)), sems(3)],
        name="outputs",
    )(both)
    return load_t.T, base_t.T


def solution(mesh):
    placed = (P("line", "bus"), P("bus", None), P(), P(), P("line"), P("line"), P(), P())
    return jax.shard_map(
        on_device,
        mesh=mesh,
        in_specs=placed,
        out_specs=(P("line", "bus"), P("line", None)),
        check_vma=False,
    )
```

```python
import jax
import jax.numpy as jnp
from jax import lax
from jax.experimental import pallas as pl
from jax.experimental.pallas import tpu as pltpu
from jax.sharding import PartitionSpec as P

MESH = pl.DeviceIdType.MESH
HOURS = 12
HPAD = 16
KS = 64
CHUNKS = (32, 32)
OFFS = tuple(sum(CHUNKS[:i]) for i in range(len(CHUNKS)))
ROWS = tuple(2 * k for k in CHUNKS)
NCH = len(CHUNKS)


def three(v):
    a = v.astype(jnp.bfloat16)
    r = v - a.astype(jnp.float32)
    b = r.astype(jnp.bfloat16)
    c = (r - b.astype(jnp.float32)).astype(jnp.bfloat16)
    return jnp.concatenate([a, b, c], axis=0)


def dot3(parts, rhs, rows):
    d = jnp.dot(parts, rhs, preferred_element_type=jnp.float32)
    return d[0:rows] + d[rows : 2 * rows] + d[2 * rows : 3 * rows]


def lookup(table_ref, tiles, index):
    low, high = index & 127, index >> 7
    total = jnp.zeros((8, 128), jnp.int32)
    for t in range(tiles):
        row = jnp.broadcast_to(table_ref[t : t + 1, :], (8, 128))
        got = jnp.take_along_axis(row, low, axis=1, mode="promise_in_bounds")
        total = jnp.where(high == t, got, total)
    return total


def main_kernel(
    x_hbm, inject_hbm, outage_hbm, from_hbm, to_hbm, region_hbm, susc_hbm, rating_hbm,
    out_ref,
    x_ref, inject_ref, outage_ref, from_ref, to_ref, region_ref, susc_ref, rating_ref, in_sem,
    ends, efc, etc, hb, rh, ph, rch, hfull, pb, ra, q, rb, p, rc, sp, rs, inc_flow, inc_sens, s4, r4,
    h1s, h1r, h2s, h2r, h3s, h3r, s0s, s0r, s1s, s1r, s2s, s2r, s3s, s3r, s4s, s4r,
):
    b = lax.axis_index("bus")
    l = lax.axis_index("line")
    zh, x, c = b // 8, (b // 2) % 4, b % 2
    y, zl = l // 4, l % 4
    z = zh * 4 + zl
    bus_loc = x_ref.shape[1]

    loads = [
        pltpu.make_async_copy(src, dst, in_sem.at[i])
        for i, (src, dst) in enumerate((
            (x_hbm, x_ref), (inject_hbm, inject_ref), (outage_hbm, outage_ref), (from_hbm, from_ref),
            (to_hbm, to_ref), (region_hbm, region_ref), (susc_hbm, susc_ref), (rating_hbm, rating_ref),
        ))
    ]
    for load in loads:
        load.start()

    def at(zh_, x_, c_, y_, zl_):
        return {"bus": (zh_ * 4 + x_) * 2 + c_, "line": y_ * 4 + zl_}

    group = [((x + dx) % 4, (c + dc) % 2) for dx in range(4) for dc in range(2) if dx or dc]

    barrier = pltpu.get_barrier_semaphore()
    for dz in range(1, 8):
        pz = (z + dz) % 8
        pl.semaphore_signal(barrier, 1, device_id=at(pz // 4, x, c, y, pz % 4), device_id_type=MESH)
    for gx, gc in group:
        pl.semaphore_signal(barrier, 1, device_id=at(zh, gx, gc, y, zl), device_id_type=MESH)
    for dy in range(1, 4):
        pl.semaphore_signal(barrier, 1, device_id=at(zh, x, c, (y + dy) % 4, zl), device_id_type=MESH)

    started = []

    def start(src, dst, ss, rs_, where):
        copy = pltpu.make_async_remote_copy(
            src_ref=src, dst_ref=dst, send_sem=ss, recv_sem=rs_, device_id=where, device_id_type=MESH
        )
        copy.start()
        started.append(copy)

    def arrived(src, dst, ss, rs_):
        pltpu.make_async_remote_copy(
            src_ref=src, dst_ref=dst, send_sem=ss, recv_sem=rs_,
            device_id=at(zh, x, 1 - c, y, zl), device_id_type=MESH,
        ).wait_recv()

    for load in loads[2:]:
        load.wait()
    rf = lookup(from_ref, 32, outage_ref[...])
    rt = lookup(to_ref, 32, outage_ref[...])
    ends[0] = rf
    ends[1] = rt
    bus_from = lookup(region_ref, 16, rf) - b * bus_loc
    bus_to = lookup(region_ref, 16, rt) - b * bus_loc
    bus_from = jnp.where((bus_from >= 0) & (bus_from < bus_loc), bus_from, -512)
    bus_to = jnp.where((bus_to >= 0) & (bus_to < bus_loc), bus_to, -512)

    lane = lax.broadcasted_iota(jnp.int32, (128, 128), 1)
    for s in range(8):
        efc[s] = (jnp.broadcast_to(bus_from[s : s + 1, :], (128, 128)).T - lane).astype(jnp.int16)
        etc[s] = (jnp.broadcast_to(bus_to[s : s + 1, :], (128, 128)).T - lane).astype(jnp.int16)

    for load in loads[:2]:
        load.wait()
    spread = lax.dot_general(
        inject_ref[...], x_ref[...], (((1,), (1,)), ((), ())), preferred_element_type=jnp.float32
    )
    zero4 = jnp.zeros((HPAD - HOURS, 128), jnp.float32)
    for xd in range(4):
        for cd in range(2):
            first = (xd * 2 + cd) * HOURS
            hb[cd, xd] = jnp.concatenate([spread[first : first + HOURS], zero4], axis=0)


    def hours2():
        rh[x * 2 + c] = hb[c, x]
        for i in range(7):
            fx, fc = (x + 4 - (i + 1) // 2) % 4, (c + (i + 1) % 2) % 2
            arrived(hb.at[0, 0], rh.at[fx * 2 + fc], h1s.at[i], h1r.at[i])
        total = ((rh[0] + rh[1]) + (rh[2] + rh[3])) + ((rh[4] + rh[5]) + (rh[6] + rh[7]))
        mine = jnp.where(zh == 0, 1.0, 0.0) * susc_ref[...]
        ph[...] = jnp.concatenate([total[0:HOURS], mine, jnp.zeros((2, 128), jnp.float32)], axis=0)
        for dz in (4, 3, 5, 2, 6, 1, 7):
            pz = (z + dz) % 8
            start(ph, rch.at[z], h2s.at[dz], h2r.at[dz], at(pz // 4, x, c, y, pz % 4))

    def hours3():
        rch[z] = ph[...]
        for dz in (1, 7, 2, 6, 3, 5, 4):
            fz = (z + 8 - dz) % 8
            arrived(ph, rch.at[fz], h2s.at[dz], h2r.at[dz])
        hfull[y] = rch[0:4] + rch[4:8]
        for dy in (2, 1, 3):
            py = (y + dy) % 4
            start(hfull.at[y], hfull.at[y], h3s.at[dy], h3r.at[dy], at(zh, x, c, py, zl))

    one = jnp.bfloat16(1.0)
    minus = jnp.bfloat16(-1.0)
    zero = jnp.bfloat16(0.0)
    step = 1024

    def select(ch, cd):
        k = CHUNKS[ch]
        at_row = pl.multiple_of(cd * 64 + OFFS[ch], 16)
        ef = jnp.concatenate([efc[zd * 4 + xd, pl.ds(at_row, k), :] for xd in range(4) for zd in range(2)], axis=0)
        et = jnp.concatenate([etc[zd * 4 + xd, pl.ds(at_row, k), :] for xd in range(4) for zd in range(2)], axis=0)
        acc = jnp.zeros((8 * k, 128), jnp.float32)
        for t in range(bus_loc // step):
            cols = []
            for u in range(step // 128):
                here = jnp.int16(t * step + u * 128)
                cols.append(jnp.where(ef == here, one, jnp.where(et == here, minus, zero)))
            acc = acc + lax.dot_general(
                jnp.concatenate(cols, axis=1), x_ref[:, t * step : (t + 1) * step],
                (((1,), (1,)), ((), ())), preferred_element_type=jnp.float32,
            )
        for xd in range(4):
            pb[ch][cd, xd, 0 : 2 * k, :] = acc[xd * 2 * k : (xd + 1) * 2 * k]

    def send0(ch):
        start(pb[ch].at[1 - c], ra[ch], s0s.at[ch], s0r.at[ch], at(zh, x, 1 - c, y, zl))

    def send1(ch):
        arrived(pb[ch].at[1 - c], ra[ch], s0s.at[ch], s0r.at[ch])
        q[ch][...] = pb[ch][c] + ra[ch][...]
        for dx in (2, 1, 3):
            px = (x + dx) % 4
            start(q[ch].at[px], rb[ch].at[x], s1s.at[ch, dx], s1r.at[ch, dx], at(zh, px, c, y, zl))

    def send2(ch):
        k = CHUNKS[ch]
        rb[ch][x] = q[ch][x]
        for dx in (1, 3, 2):
            fx = (x + 4 - dx) % 4
            arrived(q[ch].at[fx], rb[ch].at[fx], s1s.at[ch, dx], s1r.at[ch, dx])
        total = (rb[ch][0] + rb[ch][1]) + (rb[ch][2] + rb[ch][3])
        for zd in range(2):
            p[ch][zd, 0:k, :] = total[zd * k : (zd + 1) * k]
        for dz in (4, 3, 5, 2, 6, 1, 7):
            pz = (z + dz) % 8
            start(p[ch].at[pz // 4], rc[ch].at[z], s2s.at[ch, dz], s2r.at[ch, dz], at(pz // 4, x, c, y, pz % 4))

    def send3(ch):
        k = CHUNKS[ch]
        rc[ch][z] = p[ch][zh]
        for dz in (1, 7, 2, 6, 3, 5, 4):
            fz = (z + 8 - dz) % 8
            arrived(p[ch].at[0], rc[ch].at[fz], s2s.at[ch, dz], s2r.at[ch, dz])
        rows = three(jnp.concatenate([rc[ch][i, 0:k, :] + rc[ch][4 + i, 0:k, :] for i in range(4)], axis=1))
        part = dot3(rows, inc_sens[...], k)
        for py in range(4):
            sp[ch][py, 0:k, :] = part[:, py * 256 : (py + 1) * 256]
        diag = (
            lax.broadcasted_iota(jnp.int32, (k, 128), 1)
            == lax.broadcasted_iota(jnp.int32, (k, 128), 0) + (c * KS + OFFS[ch])
        )
        own = jnp.sum(jnp.where(diag, part[:, 1024:1152], 0.0), axis=0, keepdims=True)
        own = jnp.broadcast_to(jnp.concatenate([own, own], axis=1), (8, 256))
        for py in range(4):
            sp[ch][py, k : k + 8, :] = own
        for dy in (2, 1, 3):
            py = (y + dy) % 4
            start(sp[ch].at[py], rs[ch].at[y], s3s.at[ch, dy], s3r.at[ch, dy], at(zh, x, c, py, zl))
        rs[ch][y] = sp[ch][y]

    def hot(from_row, to_row, first):
        sub = lax.broadcasted_iota(jnp.int32, (128, 128), 0) + first
        return (
            (jnp.broadcast_to(from_row, (128, 128)) - sub).astype(jnp.int16),
            (jnp.broadcast_to(to_row, (128, 128)) - sub).astype(jnp.int16),
        )

    def fill(out, g, tiles, from_row, to_row, first):
        f16, t16 = hot(from_row, to_row, first)
        for r in range(tiles):
            here = jnp.int16(r * 128)
            out[r * 128 : (r + 1) * 128, g * 128 : (g + 1) * 128] = jnp.where(
                f16 == here, one, jnp.where(t16 == here, minus, zero)
            )

    select(0, 1 - c)
    pl.semaphore_wait(barrier, 17)
    send0(0)
    for i, (gx, gc) in enumerate(group):
        start(hb.at[gc, gx], rh.at[x * 2 + c], h1s.at[i], h1r.at[i], at(zh, gx, gc, y, zl))
    select(0, c)
    send1(0)
    for ch in range(1, NCH):
        select(ch, 1 - c)
        send0(ch)
        if ch == 1:
            hours2()
        select(ch, c)
        send1(ch)
    if NCH == 1:
        hours2()

    for g in range(8):
        at_line = (g // 2 * 4 + zl) * 2 + g % 2
        fill(inc_sens, g, 4, from_ref[pl.ds(at_line, 1), :], to_ref[pl.ds(at_line, 1), :], y * 512)
    at_tile = zh * 4 + x
    fill(inc_sens, 8, 4, ends[0, pl.ds(at_tile, 1), :], ends[1, pl.ds(at_tile, 1), :], y * 512)
    send2(0)
    for g in range(2):
        fill(inc_flow, g, 16, from_ref[pl.ds(l * 2 + g, 1), :], to_ref[pl.ds(l * 2 + g, 1), :], 0)
    for g in range(4):
        fill(inc_flow, 2 + g, 16, ends[0, pl.ds(zh * 4 + g, 1), :], ends[1, pl.ds(zh * 4 + g, 1), :], 0)
    hours3()
    for ch in range(1, NCH):
        send2(ch)
    for ch in range(NCH - 1):
        send3(ch)

    susc_row = jnp.concatenate([susc_ref[0:1, :], susc_ref[1:2, :]], axis=1)
    for dy in (1, 3, 2):
        fy = (y + 4 - dy) % 4
        arrived(hfull.at[y], hfull.at[fy], h3s.at[dy], h3r.at[dy])
    hours = jnp.concatenate([hfull[i // 4, i % 4] for i in range(16)], axis=1)
    flows = dot3(three(hours), inc_flow[...], HPAD)
    own_flow = flows[:, 0:256] * susc_row
    for xd in range(4):
        s4[xd, :, 0:256] = own_flow
        s4[xd, :, 256:384] = flows[:, 256 + xd * 128 : 384 + xd * 128]
    for i, (gx, gc) in enumerate(group):
        start(s4.at[gx], r4.at[x * 2 + c], s4s.at[i], s4r.at[i], at(zh, gx, gc, y, zl))
    r4[x * 2 + c] = s4[x]
    send3(NCH - 1)

    row = outage_ref[pl.ds(at_tile, 1), :]
    table = jnp.concatenate([hfull[i // 4, i % 4, HOURS : HOURS + 2, :] for i in range(16)], axis=0)
    low = jnp.broadcast_to(row & 127, (128, 128))
    hit = jnp.where(low == lax.broadcasted_iota(jnp.int32, (128, 128), 0), 1.0, 0.0).astype(jnp.bfloat16)
    cand = dot3(three(table), hit, 32)
    high = jnp.broadcast_to(row >> 7, (32, 128))
    susc_out = jnp.sum(
        jnp.where(high == lax.broadcasted_iota(jnp.int32, (32, 128), 0), cand, 0.0), axis=0, keepdims=True
    )

    for i in range(7):
        fx, fc = (x + 4 - (i + 1) // 2) % 4, (c + (i + 1) % 2) % 2
        arrived(s4.at[0], r4.at[fx * 2 + fc], s4s.at[i], s4r.at[i])
    outflow = r4[:, :, 256:384].reshape(128, 128) * susc_out
    outflow = outflow.T
    outflow = jnp.where(c == 0, outflow[0:KS], outflow[KS : 2 * KS])
    rating_row = jnp.concatenate([rating_ref[0:1, :], rating_ref[1:2, :]], axis=1)
    for s in range(8):
        out_ref[KS + s * HOURS : KS + (s + 1) * HOURS, :] = r4[s, 0:HOURS, 0:256]
    for ch in range(NCH):
        k, first = CHUNKS[ch], OFFS[ch]
        for dy in (1, 3, 2):
            fy = (y + 4 - dy) % 4
            arrived(sp[ch].at[0], rs[ch].at[fy], s3s.at[ch, dy], s3r.at[ch, dy])
        total = (rs[ch][0] + rs[ch][1]) + (rs[ch][2] + rs[ch][3])
        divisor = jnp.maximum(1.0 - total[k : k + 1, 0:128] * susc_out, 0.25)
        here = (
            lax.broadcasted_iota(jnp.int32, (k, 128), 1)
            == lax.broadcasted_iota(jnp.int32, (k, 128), 0) + (c * KS + first)
        )
        divisor = jnp.sum(jnp.where(here, jnp.broadcast_to(divisor, (k, 128)), 0.0), axis=1, keepdims=True)
        ratio = total[0:k] * susc_row / divisor
        worst = jnp.zeros((k, 256), jnp.float32)
        for s in range(8):
            for h in range(HOURS):
                flow = r4[s, h : h + 1, 0:256]
                col = outflow[first : first + k, s * HPAD + h : s * HPAD + h + 1]
                worst = jnp.maximum(worst, jnp.abs(flow + ratio * col))
        out_ref[first : first + k, :] = worst / rating_row

    for copy in started:
        copy.wait_send()


def split_kernel(both_ref, load_ref, base_ref, here, sem):
    load = pltpu.make_async_copy(both_ref, here, sem.at[2])
    load.start()
    load.wait()
    first = pltpu.make_async_copy(here.at[0:KS, :], load_ref, sem.at[0])
    second = pltpu.make_async_copy(here.at[KS : KS + 96, :], base_ref, sem.at[1])
    first.start()
    second.start()
    first.wait()
    second.wait()


def on_device(xrows, inject, line_from, line_to, suscept, rating, region_bus, outage):
    vm = pl.BlockSpec(memory_space=pltpu.VMEM)
    far = pl.BlockSpec(memory_space=pl.ANY)
    f32, bf16, i16, i32 = jnp.float32, jnp.bfloat16, jnp.int16, jnp.int32
    vmem = lambda shape, kind=f32: pltpu.VMEM(shape, kind)
    each = lambda lead, counts, last=128: tuple(pltpu.VMEM(lead + (n, last), f32) for n in counts)
    sems = lambda *shape: pltpu.SemaphoreType.DMA(shape)
    args = (
        xrows, inject.T, outage.reshape(8, 128), line_from.reshape(32, 128), line_to.reshape(32, 128),
        region_bus.reshape(16, 128), suscept.reshape(2, 128), rating.reshape(2, 128),
    )
    sens_rows = tuple(k + 8 for k in CHUNKS)
    both = pl.pallas_call(
        main_kernel,
        out_shape=jax.ShapeDtypeStruct((KS + 96, 256), f32),
        in_specs=[far] * 8,
        out_specs=vm,
        scratch_shapes=[
            *[vmem(a.shape, a.dtype) for a in args],
            sems(8),
            vmem((2, 8, 128), i32),
            vmem((8, 128, 128), i16),
            vmem((8, 128, 128), i16),
            vmem((2, 4, HPAD, 128)),
            vmem((8, HPAD, 128)),
            vmem((HPAD, 128)),
            vmem((8, HPAD, 128)),
            vmem((4, 4, HPAD, 128)),
            each((2, 4), ROWS),
            each((4,), ROWS),
            each((4,), ROWS),
            each((4,), ROWS),
            each((2,), CHUNKS),
            each((8,), CHUNKS),
            each((4,), sens_rows, 256),
            each((4,), sens_rows, 256),
            vmem((2048, 768), bf16),
            vmem((512, 1152), bf16),
            vmem((4, HPAD, 384)),
            vmem((8, HPAD, 384)),
            sems(7), sems(7),
            sems(8), sems(8),
            sems(4), sems(4),
            sems(NCH), sems(NCH),
            sems(NCH, 4), sems(NCH, 4),
            sems(NCH, 8), sems(NCH, 8),
            sems(NCH, 4), sems(NCH, 4),
            sems(7), sems(7),
        ],
        compiler_params=pltpu.CompilerParams(
            collective_id=0, has_side_effects=True, vmem_limit_bytes=60 * 1024 * 1024
        ),
        name="exchange",
    )(*args)
    load_t, base_t = pl.pallas_call(
        split_kernel,
        out_shape=(jax.ShapeDtypeStruct((KS, 256), f32), jax.ShapeDtypeStruct((96, 256), f32)),
        in_specs=[far],
        out_specs=(far, far),
        scratch_shapes=[vmem((KS + 96, 256)), sems(3)],
        name="outputs",
    )(both)
    return load_t.T, base_t.T


def solution(mesh):
    placed = (P("line", "bus"), P("bus", None), P(), P(), P("line"), P("line"), P(), P())
    return jax.shard_map(
        on_device,
        mesh=mesh,
        in_specs=placed,
        out_specs=(P("line", "bus"), P("line", None)),
        check_vma=False,
    )
```

```python
import jax
import jax.numpy as jnp
from jax import lax
from jax.experimental import pallas as pl
from jax.experimental.pallas import tpu as pltpu
from jax.sharding import PartitionSpec as P

MESH = pl.DeviceIdType.MESH
HOURS = 12
HPAD = 16
KS = 64
CHUNKS = (32, 32)
OFFS = tuple(sum(CHUNKS[:i]) for i in range(len(CHUNKS)))
ROWS = tuple(2 * k for k in CHUNKS)
NCH = len(CHUNKS)


def three(v):
    a = v.astype(jnp.bfloat16)
    r = v - a.astype(jnp.float32)
    b = r.astype(jnp.bfloat16)
    c = (r - b.astype(jnp.float32)).astype(jnp.bfloat16)
    return jnp.concatenate([a, b, c], axis=0)


def dot3(parts, rhs, rows):
    d = jnp.dot(parts, rhs, preferred_element_type=jnp.float32)
    return d[0:rows] + d[rows : 2 * rows] + d[2 * rows : 3 * rows]


def lookup(table_ref, tiles, index):
    low, high = index & 127, index >> 7
    total = jnp.zeros((8, 128), jnp.int32)
    for t in range(tiles):
        row = jnp.broadcast_to(table_ref[t : t + 1, :], (8, 128))
        got = jnp.take_along_axis(row, low, axis=1, mode="promise_in_bounds")
        total = jnp.where(high == t, got, total)
    return total


def main_kernel(
    x_hbm, inject_hbm, outage_hbm, from_hbm, to_hbm, region_hbm, susc_hbm, rating_hbm,
    out_hbm,
    x_ref, inject_ref, outage_ref, from_ref, to_ref, region_ref, susc_ref, rating_ref, in_sem, out_ref, out_sem,
    ends, efc, etc, hb, rh, ph, rch, hfull, pb, ra, q, rb, p, rc, sp, rs, inc_flow, inc_sens, s4, r4,
    h1s, h1r, h2s, h2r, h3s, h3r, s0s, s0r, s1s, s1r, s2s, s2r, s3s, s3r, s4s, s4r,
):
    b = lax.axis_index("bus")
    l = lax.axis_index("line")
    zh, x, c = b // 8, (b // 2) % 4, b % 2
    y, zl = l // 4, l % 4
    z = zh * 4 + zl
    bus_loc = x_ref.shape[1]

    loads = [
        pltpu.make_async_copy(src, dst, in_sem.at[i])
        for i, (src, dst) in enumerate((
            (x_hbm, x_ref), (inject_hbm, inject_ref), (outage_hbm, outage_ref), (from_hbm, from_ref),
            (to_hbm, to_ref), (region_hbm, region_ref), (susc_hbm, susc_ref), (rating_hbm, rating_ref),
        ))
    ]
    for load in loads:
        load.start()

    def at(zh_, x_, c_, y_, zl_):
        return {"bus": (zh_ * 4 + x_) * 2 + c_, "line": y_ * 4 + zl_}

    group = [((x + dx) % 4, (c + dc) % 2) for dx in range(4) for dc in range(2) if dx or dc]

    barrier = pltpu.get_barrier_semaphore()
    for dz in range(1, 8):
        pz = (z + dz) % 8
        pl.semaphore_signal(barrier, 1, device_id=at(pz // 4, x, c, y, pz % 4), device_id_type=MESH)
    for gx, gc in group:
        pl.semaphore_signal(barrier, 1, device_id=at(zh, gx, gc, y, zl), device_id_type=MESH)
    for dy in range(1, 4):
        pl.semaphore_signal(barrier, 1, device_id=at(zh, x, c, (y + dy) % 4, zl), device_id_type=MESH)

    started = []

    def start(src, dst, ss, rs_, where):
        copy = pltpu.make_async_remote_copy(
            src_ref=src, dst_ref=dst, send_sem=ss, recv_sem=rs_, device_id=where, device_id_type=MESH
        )
        copy.start()
        started.append(copy)

    def arrived(src, dst, ss, rs_):
        pltpu.make_async_remote_copy(
            src_ref=src, dst_ref=dst, send_sem=ss, recv_sem=rs_,
            device_id=at(zh, x, 1 - c, y, zl), device_id_type=MESH,
        ).wait_recv()

    for load in loads[2:]:
        load.wait()
    rf = lookup(from_ref, 32, outage_ref[...])
    rt = lookup(to_ref, 32, outage_ref[...])
    ends[0] = rf
    ends[1] = rt
    bus_from = lookup(region_ref, 16, rf) - b * bus_loc
    bus_to = lookup(region_ref, 16, rt) - b * bus_loc
    bus_from = jnp.where((bus_from >= 0) & (bus_from < bus_loc), bus_from, -512)
    bus_to = jnp.where((bus_to >= 0) & (bus_to < bus_loc), bus_to, -512)

    lane = lax.broadcasted_iota(jnp.int32, (128, 128), 1)
    for s in range(8):
        efc[s] = (jnp.broadcast_to(bus_from[s : s + 1, :], (128, 128)).T - lane).astype(jnp.int16)
        etc[s] = (jnp.broadcast_to(bus_to[s : s + 1, :], (128, 128)).T - lane).astype(jnp.int16)

    for load in loads[:2]:
        load.wait()
    spread = lax.dot_general(
        inject_ref[...], x_ref[...], (((1,), (1,)), ((), ())), preferred_element_type=jnp.float32
    )
    zero4 = jnp.zeros((HPAD - HOURS, 128), jnp.float32)
    for xd in range(4):
        for cd in range(2):
            first = (xd * 2 + cd) * HOURS
            hb[cd, xd] = jnp.concatenate([spread[first : first + HOURS], zero4], axis=0)


    def hours2():
        rh[x * 2 + c] = hb[c, x]
        for i in range(7):
            fx, fc = (x + 4 - (i + 1) // 2) % 4, (c + (i + 1) % 2) % 2
            arrived(hb.at[0, 0], rh.at[fx * 2 + fc], h1s.at[i], h1r.at[i])
        total = ((rh[0] + rh[1]) + (rh[2] + rh[3])) + ((rh[4] + rh[5]) + (rh[6] + rh[7]))
        mine = jnp.where(zh == 0, 1.0, 0.0) * susc_ref[...]
        ph[...] = jnp.concatenate([total[0:HOURS], mine, jnp.zeros((2, 128), jnp.float32)], axis=0)
        for dz in (4, 3, 5, 2, 6, 1, 7):
            pz = (z + dz) % 8
            start(ph, rch.at[z], h2s.at[dz], h2r.at[dz], at(pz // 4, x, c, y, pz % 4))

    def hours3():
        rch[z] = ph[...]
        for dz in (1, 7, 2, 6, 3, 5, 4):
            fz = (z + 8 - dz) % 8
            arrived(ph, rch.at[fz], h2s.at[dz], h2r.at[dz])
        hfull[y] = rch[0:4] + rch[4:8]
        for dy in (2, 1, 3):
            py = (y + dy) % 4
            start(hfull.at[y], hfull.at[y], h3s.at[dy], h3r.at[dy], at(zh, x, c, py, zl))

    one = jnp.bfloat16(1.0)
    minus = jnp.bfloat16(-1.0)
    zero = jnp.bfloat16(0.0)
    step = 1024

    def select(ch, cd):
        k = CHUNKS[ch]
        at_row = pl.multiple_of(cd * 64 + OFFS[ch], 16)
        ef = jnp.concatenate([efc[zd * 4 + xd, pl.ds(at_row, k), :] for xd in range(4) for zd in range(2)], axis=0)
        et = jnp.concatenate([etc[zd * 4 + xd, pl.ds(at_row, k), :] for xd in range(4) for zd in range(2)], axis=0)
        acc = jnp.zeros((8 * k, 128), jnp.float32)
        for t in range(bus_loc // step):
            cols = []
            for u in range(step // 128):
                here = jnp.int16(t * step + u * 128)
                cols.append(jnp.where(ef == here, one, jnp.where(et == here, minus, zero)))
            acc = acc + lax.dot_general(
                jnp.concatenate(cols, axis=1), x_ref[:, t * step : (t + 1) * step],
                (((1,), (1,)), ((), ())), preferred_element_type=jnp.float32,
            )
        for xd in range(4):
            pb[ch][cd, xd, 0 : 2 * k, :] = acc[xd * 2 * k : (xd + 1) * 2 * k]

    def send0(ch):
        start(pb[ch].at[1 - c], ra[ch], s0s.at[ch], s0r.at[ch], at(zh, x, 1 - c, y, zl))

    def send1(ch):
        arrived(pb[ch].at[1 - c], ra[ch], s0s.at[ch], s0r.at[ch])
        q[ch][...] = pb[ch][c] + ra[ch][...]
        for dx in (2, 1, 3):
            px = (x + dx) % 4
            start(q[ch].at[px], rb[ch].at[x], s1s.at[ch, dx], s1r.at[ch, dx], at(zh, px, c, y, zl))

    def send2(ch):
        k = CHUNKS[ch]
        rb[ch][x] = q[ch][x]
        for dx in (1, 3, 2):
            fx = (x + 4 - dx) % 4
            arrived(q[ch].at[fx], rb[ch].at[fx], s1s.at[ch, dx], s1r.at[ch, dx])
        total = (rb[ch][0] + rb[ch][1]) + (rb[ch][2] + rb[ch][3])
        for zd in range(2):
            p[ch][zd, 0:k, :] = total[zd * k : (zd + 1) * k]
        for dz in (4, 3, 5, 2, 6, 1, 7):
            pz = (z + dz) % 8
            start(p[ch].at[pz // 4], rc[ch].at[z], s2s.at[ch, dz], s2r.at[ch, dz], at(pz // 4, x, c, y, pz % 4))

    def send3(ch):
        k = CHUNKS[ch]
        rc[ch][z] = p[ch][zh]
        for dz in (1, 7, 2, 6, 3, 5, 4):
            fz = (z + 8 - dz) % 8
            arrived(p[ch].at[0], rc[ch].at[fz], s2s.at[ch, dz], s2r.at[ch, dz])
        rows = three(jnp.concatenate([rc[ch][i, 0:k, :] + rc[ch][4 + i, 0:k, :] for i in range(4)], axis=1))
        part = dot3(rows, inc_sens[...], k)
        for py in range(4):
            sp[ch][py, 0:k, :] = part[:, py * 256 : (py + 1) * 256]
        diag = (
            lax.broadcasted_iota(jnp.int32, (k, 128), 1)
            == lax.broadcasted_iota(jnp.int32, (k, 128), 0) + (c * KS + OFFS[ch])
        )
        own = jnp.sum(jnp.where(diag, part[:, 1024:1152], 0.0), axis=0, keepdims=True)
        own = jnp.broadcast_to(jnp.concatenate([own, own], axis=1), (8, 256))
        for py in range(4):
            sp[ch][py, k : k + 8, :] = own
        for dy in (2, 1, 3):
            py = (y + dy) % 4
            start(sp[ch].at[py], rs[ch].at[y], s3s.at[ch, dy], s3r.at[ch, dy], at(zh, x, c, py, zl))
        rs[ch][y] = sp[ch][y]

    def hot(from_row, to_row, first):
        sub = lax.broadcasted_iota(jnp.int32, (128, 128), 0) + first
        return (
            (jnp.broadcast_to(from_row, (128, 128)) - sub).astype(jnp.int16),
            (jnp.broadcast_to(to_row, (128, 128)) - sub).astype(jnp.int16),
        )

    def fill(out, g, tiles, from_row, to_row, first):
        f16, t16 = hot(from_row, to_row, first)
        for r in range(tiles):
            here = jnp.int16(r * 128)
            out[r * 128 : (r + 1) * 128, g * 128 : (g + 1) * 128] = jnp.where(
                f16 == here, one, jnp.where(t16 == here, minus, zero)
            )

    select(0, 1 - c)
    pl.semaphore_wait(barrier, 17)
    send0(0)
    for i, (gx, gc) in enumerate(group):
        start(hb.at[gc, gx], rh.at[x * 2 + c], h1s.at[i], h1r.at[i], at(zh, gx, gc, y, zl))
    select(0, c)
    send1(0)
    for ch in range(1, NCH):
        select(ch, 1 - c)
        send0(ch)
        if ch == 1:
            hours2()
        select(ch, c)
        send1(ch)
    if NCH == 1:
        hours2()

    for g in range(8):
        at_line = (g // 2 * 4 + zl) * 2 + g % 2
        fill(inc_sens, g, 4, from_ref[pl.ds(at_line, 1), :], to_ref[pl.ds(at_line, 1), :], y * 512)
    at_tile = zh * 4 + x
    fill(inc_sens, 8, 4, ends[0, pl.ds(at_tile, 1), :], ends[1, pl.ds(at_tile, 1), :], y * 512)
    send2(0)
    for g in range(2):
        fill(inc_flow, g, 16, from_ref[pl.ds(l * 2 + g, 1), :], to_ref[pl.ds(l * 2 + g, 1), :], 0)
    for g in range(4):
        fill(inc_flow, 2 + g, 16, ends[0, pl.ds(zh * 4 + g, 1), :], ends[1, pl.ds(zh * 4 + g, 1), :], 0)
    hours3()
    for ch in range(1, NCH):
        send2(ch)
    for ch in range(NCH - 1):
        send3(ch)

    susc_row = jnp.concatenate([susc_ref[0:1, :], susc_ref[1:2, :]], axis=1)
    for dy in (1, 3, 2):
        fy = (y + 4 - dy) % 4
        arrived(hfull.at[y], hfull.at[fy], h3s.at[dy], h3r.at[dy])
    hours = jnp.concatenate([hfull[i // 4, i % 4] for i in range(16)], axis=1)
    flows = dot3(three(hours), inc_flow[...], HPAD)
    own_flow = flows[:, 0:256] * susc_row
    for xd in range(4):
        s4[xd, :, 0:256] = own_flow
        s4[xd, :, 256:384] = flows[:, 256 + xd * 128 : 384 + xd * 128]
    for i, (gx, gc) in enumerate(group):
        start(s4.at[gx], r4.at[x * 2 + c], s4s.at[i], s4r.at[i], at(zh, gx, gc, y, zl))
    r4[x * 2 + c] = s4[x]
    send3(NCH - 1)

    row = outage_ref[pl.ds(at_tile, 1), :]
    table = jnp.concatenate([hfull[i // 4, i % 4, HOURS : HOURS + 2, :] for i in range(16)], axis=0)
    low = jnp.broadcast_to(row & 127, (128, 128))
    hit = jnp.where(low == lax.broadcasted_iota(jnp.int32, (128, 128), 0), 1.0, 0.0).astype(jnp.bfloat16)
    cand = dot3(three(table), hit, 32)
    high = jnp.broadcast_to(row >> 7, (32, 128))
    susc_out = jnp.sum(
        jnp.where(high == lax.broadcasted_iota(jnp.int32, (32, 128), 0), cand, 0.0), axis=0, keepdims=True
    )

    for i in range(7):
        fx, fc = (x + 4 - (i + 1) // 2) % 4, (c + (i + 1) % 2) % 2
        arrived(s4.at[0], r4.at[fx * 2 + fc], s4s.at[i], s4r.at[i])
    outflow = r4[:, :, 256:384].reshape(128, 128) * susc_out
    outflow = outflow.T
    outflow = jnp.where(c == 0, outflow[0:KS], outflow[KS : 2 * KS])
    rating_row = jnp.concatenate([rating_ref[0:1, :], rating_ref[1:2, :]], axis=1)
    for s in range(8):
        out_ref[KS + s * HOURS : KS + (s + 1) * HOURS, :] = r4[s, 0:HOURS, 0:256]
    stores = [pltpu.make_async_copy(out_ref.at[KS : KS + 96, :], out_hbm.at[KS : KS + 96, :], out_sem.at[NCH])]
    stores[0].start()
    for ch in range(NCH):
        k, first = CHUNKS[ch], OFFS[ch]
        for dy in (1, 3, 2):
            fy = (y + 4 - dy) % 4
            arrived(sp[ch].at[0], rs[ch].at[fy], s3s.at[ch, dy], s3r.at[ch, dy])
        total = (rs[ch][0] + rs[ch][1]) + (rs[ch][2] + rs[ch][3])
        divisor = jnp.maximum(1.0 - total[k : k + 1, 0:128] * susc_out, 0.25)
        here = (
            lax.broadcasted_iota(jnp.int32, (k, 128), 1)
            == lax.broadcasted_iota(jnp.int32, (k, 128), 0) + (c * KS + first)
        )
        divisor = jnp.sum(jnp.where(here, jnp.broadcast_to(divisor, (k, 128)), 0.0), axis=1, keepdims=True)
        ratio = total[0:k] * susc_row / divisor
        worst = jnp.zeros((k, 256), jnp.float32)
        for s in range(8):
            for h in range(HOURS):
                flow = r4[s, h : h + 1, 0:256]
                col = outflow[first : first + k, s * HPAD + h : s * HPAD + h + 1]
                worst = jnp.maximum(worst, jnp.abs(flow + ratio * col))
        out_ref[first : first + k, :] = worst / rating_row
        rows = pl.ds(first, k)
        stores.append(pltpu.make_async_copy(out_ref.at[rows, :], out_hbm.at[rows, :], out_sem.at[ch]))
        stores[-1].start()

    for copy in started:
        copy.wait_send()
    for store in stores:
        store.wait()


def split_kernel(both_ref, load_ref, base_ref, here, sem):
    load = pltpu.make_async_copy(both_ref, here, sem.at[2])
    load.start()
    load.wait()
    first = pltpu.make_async_copy(here.at[0:KS, :], load_ref, sem.at[0])
    second = pltpu.make_async_copy(here.at[KS : KS + 96, :], base_ref, sem.at[1])
    first.start()
    second.start()
    first.wait()
    second.wait()


def on_device(xrows, inject, line_from, line_to, suscept, rating, region_bus, outage):
    far = pl.BlockSpec(memory_space=pl.ANY)
    f32, bf16, i16, i32 = jnp.float32, jnp.bfloat16, jnp.int16, jnp.int32
    vmem = lambda shape, kind=f32: pltpu.VMEM(shape, kind)
    each = lambda lead, counts, last=128: tuple(pltpu.VMEM(lead + (n, last), f32) for n in counts)
    sems = lambda *shape: pltpu.SemaphoreType.DMA(shape)
    args = (
        xrows, inject.T, outage.reshape(8, 128), line_from.reshape(32, 128), line_to.reshape(32, 128),
        region_bus.reshape(16, 128), suscept.reshape(2, 128), rating.reshape(2, 128),
    )
    sens_rows = tuple(k + 8 for k in CHUNKS)
    both = pl.pallas_call(
        main_kernel,
        out_shape=jax.ShapeDtypeStruct((KS + 96, 256), f32),
        in_specs=[far] * 8,
        out_specs=far,
        scratch_shapes=[
            *[vmem(a.shape, a.dtype) for a in args],
            sems(8),
            vmem((KS + 96, 256)),
            sems(NCH + 1),
            vmem((2, 8, 128), i32),
            vmem((8, 128, 128), i16),
            vmem((8, 128, 128), i16),
            vmem((2, 4, HPAD, 128)),
            vmem((8, HPAD, 128)),
            vmem((HPAD, 128)),
            vmem((8, HPAD, 128)),
            vmem((4, 4, HPAD, 128)),
            each((2, 4), ROWS),
            each((4,), ROWS),
            each((4,), ROWS),
            each((4,), ROWS),
            each((2,), CHUNKS),
            each((8,), CHUNKS),
            each((4,), sens_rows, 256),
            each((4,), sens_rows, 256),
            vmem((2048, 768), bf16),
            vmem((512, 1152), bf16),
            vmem((4, HPAD, 384)),
            vmem((8, HPAD, 384)),
            sems(7), sems(7),
            sems(8), sems(8),
            sems(4), sems(4),
            sems(NCH), sems(NCH),
            sems(NCH, 4), sems(NCH, 4),
            sems(NCH, 8), sems(NCH, 8),
            sems(NCH, 4), sems(NCH, 4),
            sems(7), sems(7),
        ],
        compiler_params=pltpu.CompilerParams(
            collective_id=0, has_side_effects=True, vmem_limit_bytes=60 * 1024 * 1024
        ),
        name="exchange",
    )(*args)
    load_t, base_t = pl.pallas_call(
        split_kernel,
        out_shape=(jax.ShapeDtypeStruct((KS, 256), f32), jax.ShapeDtypeStruct((96, 256), f32)),
        in_specs=[far],
        out_specs=(far, far),
        scratch_shapes=[vmem((KS + 96, 256)), sems(3)],
        name="outputs",
    )(both)
    return load_t.T, base_t.T


def solution(mesh):
    placed = (P("line", "bus"), P("bus", None), P(), P(), P("line"), P("line"), P(), P())
    return jax.shard_map(
        on_device,
        mesh=mesh,
        in_specs=placed,
        out_specs=(P("line", "bus"), P("line", None)),
        check_vma=False,
    )
```
